32 devices in a mesh: parts: 2 (over x), req: 2 (over core), tp: 8 (over z, y).
Axes of the slice: x: 2, y: 2, z: 4, core: 2. Of those that a mesh axis runs over, the one named last changes fastest.
Arguments:
- input_hidden_rows: bfloat16 [64, 8192], P(('parts', 'req')), parts along dimension 0, may hold values from -6 to 6
- input_norm_scale: bfloat16 [8192], replicated, may hold values from 0.099609375 to 1.8984375
- query_weight: bfloat16 [8192, 4096], P(None, 'tp'), may hold values from -0.0625 to 0.0625
- key_value_weight: bfloat16 [8192, 1024], P(None, 'tp'), may hold values from -0.0625 to 0.0625
- output_weight: bfloat16 [4096, 8192], P('tp'), may hold values from -0.125 to 0.125
- cache: bfloat16 [64, 512, 1024], P(('parts', 'req', 'tp')), parts along dimension 0, may hold values from -2000 to 2000
- lengths: int32 [64], P(('parts', 'req', 'tp')), parts along dimension 0, may hold values from 2 to 512, as said below
- adapter_per_block: int32 [4], P(('parts', 'req')), parts along dimension 0, may hold values from 0 to 127
- adapter_storage_slot: int32 [128], replicated, may hold values from 0 to 127, each once
- adapter_down_projection: bfloat16 [128, 16, 4096], P('req', None, 'tp'), may hold values from -0.09375 to 0.09375
- adapter_up_projection: bfloat16 [128, 16, 8192], P('req', None, 'tp'), may hold values from -3 to 3
Outputs:
- hidden_out: bfloat16 [64, 8192], P(('parts', 'req')), parts along dimension 0
- new_pairs: bfloat16 [2, 64, 1024], P(None, ('parts', 'req', 'tp')), parts along dimension 1
The draws below stay inside these ranges and needn't reach their ends.
There are 2 independent parts, one for each index of `parts`. The reference program is written for one: setup_inputs(seed, part) draws one part's arguments, and reference() takes and returns one part's arrays. A program takes and returns all parts, laid end to end along the dimension named above; an argument that names none is the same for every part. Nothing has to cross between parts.
Inputs may be any that keep to these rules, and one draw needn't show every extreme that they name: `lengths`: each row has at least two valid positions and some row of every draw has 512.
All inputs are finite; a program needn't handle non-finite values.
Results may differ from the reference program's by a relative error of at most 0.025.
The reference program's roundings to bfloat16 on the way count: a program that leaves them out, or rounds other values in their place, can miss the bound.
Values may be sent and summed in bfloat16 or wider, within the bound.
No kernel may reach another device: no remote copies, remote signals or barrier semaphores. Data moves between devices by JAX's collectives and lax.ppermute only.
A program may use at most 128 MiB of HBM per device.

```python
import math
import jax
import jax.numpy as jnp
import numpy as np
from jax import lax

MODEL_WIDTH = 8192
HEAD_SIZE = 128
QUERY_HEAD_COUNT = 32
KV_HEADS = 4
ADAPTER_RANK = 16
BLOCK = 16
STEPS = 2
CTX = 512
ROWS = 32
BLOCKS = 2
ADAPTER_COUNT = 128


def draw_cache(key, part):
    key = jax.random.fold_in(key, 11)
    first_key = jax.random.fold_in(key, 0)
    width = 2 * KV_HEADS * HEAD_SIZE
    return jnp.clip(jax.random.normal(first_key, (ROWS, CTX, width), jnp.float32), -6.0, 6.0).astype(jnp.bfloat16)


def draw_lengths(key, part):
    key = jax.random.fold_in(key, 23)
    drawn = jax.random.randint(key, (ROWS,), 2, CTX + 1)
    return jnp.where(jnp.arange(ROWS) == 0, CTX, drawn).astype(jnp.int32)


def spiked(array, stream_key, source, target, shards_of, factor):
    def block_of(dim):
        return (jnp.arange(array.shape[dim]) // (array.shape[dim] // shards_of)).reshape((-1,) + (1,) * (array.ndim - 1 - dim))

    near = jax.random.permutation(stream_key, shards_of)[block_of(target)]
    second = (block_of(target) + shards_of // 2) % shards_of
    return jnp.where((block_of(source) == near) | (block_of(source) == second), factor * array, array)


def block_levels(own_key, dims, shards, low, largest):
    loudness, own = 1.0, jax.random.fold_in(own_key, 6)
    for position, parts in shards:
        heights = jnp.exp(jax.random.uniform(jax.random.fold_in(own, position), (parts,), jnp.float32, low / len(shards), largest / len(shards)))
        loudness = loudness * jnp.repeat(heights, dims[position] // parts).reshape([-1 if axis == position else 1 for axis in range(len(dims))])
    return loudness


def cumulative_ranks(number_of, slope):
    portions = [(1 << 20) // math.isqrt(grade ** slope) + 1 for grade in range(1, number_of + 1)]
    scale = 1 + sum(portions) // (1 << 30)
    return np.cumsum(np.array([max(1, weight // scale) for weight in portions]))


def ranked_ids(rng, dims, amount, skew):
    table = cumulative_ranks(amount, skew)
    pick = jax.random.randint(jax.random.fold_in(rng, 1), dims, 0, int(table[amount - 1]))
    rank = jnp.searchsorted(jnp.asarray(table, jnp.int32), pick, side="right")
    return jax.random.permutation(jax.random.fold_in(rng, 2), amount)[rank].astype(jnp.int32)


def scatter_about(rng, dims, scale, reach, pieces=(), kind=jnp.bfloat16):
    level = block_levels(rng, dims, pieces, -0.22, 0.18) if pieces else 1.0
    array = jax.random.normal(rng, dims, jnp.float32) * scale * level
    return jnp.minimum(jnp.maximum(array, -reach), reach).astype(kind)


def bell_draw_with(key, dims, scale, reach, cuts, heavy, kind=jnp.bfloat16):
    entries = scale * jax.random.normal(key, dims, jnp.float32)
    if cuts:
        entries = entries * block_levels(key, dims, cuts, -0.22, 0.18)
    return jnp.clip(spiked(entries, jax.random.fold_in(key, 3), *heavy), -reach, reach).astype(kind)


def setup_inputs(seed: int = 0, part: int = 0) -> dict:
    key_list = jax.random.split(jax.random.key(seed), 12)
    own_keys = jax.random.split(jax.random.fold_in(key_list[11], part), 12)
    return {
        "input_hidden_rows": scatter_about(own_keys[0], (ROWS, MODEL_WIDTH), 1.0, 6.0, ((0, 2),)),
        "input_norm_scale": jnp.clip(1.0 + 0.18 * jax.random.normal(key_list[1], (MODEL_WIDTH,), jnp.float32), 0.099609375, 1.8984375).astype(jnp.bfloat16),
        "query_weight": scatter_about(key_list[2], (MODEL_WIDTH, QUERY_HEAD_COUNT * HEAD_SIZE), MODEL_WIDTH ** -0.5, 0.0625, ((1, 8),)),
        "key_value_weight": scatter_about(key_list[3], (MODEL_WIDTH, 2 * KV_HEADS * HEAD_SIZE), MODEL_WIDTH ** -0.5, 0.0625, ((1, 8),)),
        "output_weight": bell_draw_with(key_list[4], (QUERY_HEAD_COUNT * HEAD_SIZE, MODEL_WIDTH), (QUERY_HEAD_COUNT * HEAD_SIZE) ** -0.5, 0.125, ((0, 8),), (0, 1, 8, 2.0)),
        "cache": draw_cache(jax.random.fold_in(jax.random.fold_in(key_list[11], part), 71), part),
        "lengths": draw_lengths(jax.random.fold_in(jax.random.fold_in(key_list[11], part), 71), part),
        "adapter_per_block": ranked_ids(own_keys[7], (BLOCKS,), ADAPTER_COUNT, 2),
        "adapter_storage_slot": jax.random.permutation(key_list[8], ADAPTER_COUNT).astype(jnp.int32),
        "adapter_down_projection": scatter_about(key_list[9], (ADAPTER_COUNT, ADAPTER_RANK, QUERY_HEAD_COUNT * HEAD_SIZE), (QUERY_HEAD_COUNT * HEAD_SIZE) ** -0.5, 0.09375, ((0, 2), (2, 8))),
        "adapter_up_projection": scatter_about(key_list[10], (ADAPTER_COUNT, ADAPTER_RANK, MODEL_WIDTH), 0.5, 3.0, ((0, 2), (2, 8))),
    }


rope_base = 500000.0
norm_epsilon = 1e-05

def rotate(values_in, positions):
    half_dim = values_in.shape[-1] // 2
    frequency = rope_base ** (-(jnp.arange(half_dim, dtype=jnp.float32) * 2.0 / values_in.shape[-1]))
    angles = positions.astype(jnp.float32)[:, None, None] * frequency[None, None, :]
    cosine = jnp.cos(angles)
    sine_part = jnp.sin(angles)
    front_half = values_in[..., :half_dim]
    back_half = values_in[..., half_dim:]
    return jnp.concatenate([front_half * cosine - back_half * sine_part, back_half * cosine + front_half * sine_part], axis=-1)

def reference(input_hidden_rows, input_norm_scale, query_weight, key_value_weight, output_weight, cache, lengths, adapter_per_block, adapter_storage_slot, adapter_down_projection, adapter_up_projection):
    row_count = input_hidden_rows.shape[0]
    groups = QUERY_HEAD_COUNT // KV_HEADS
    half_kv = KV_HEADS * HEAD_SIZE
    slot_in_storage = adapter_storage_slot[adapter_per_block]
    down_matrices = adapter_down_projection[slot_in_storage].astype(jnp.float32)
    up_matrices = adapter_up_projection[slot_in_storage].astype(jnp.float32)
    cache_keys = cache[:, :, :half_kv].reshape(row_count, CTX, KV_HEADS, HEAD_SIZE)
    cache_values = cache[:, :, half_kv:].reshape(row_count, CTX, KV_HEADS, HEAD_SIZE)
    cache_valid = jnp.arange(CTX, dtype=jnp.int32)[None, :] < lengths[:, None]
    hidden = input_hidden_rows
    fresh_keys = []
    fresh_values = []
    stored = []
    for decode_step in range(STEPS):
        wide_hidden = hidden.astype(jnp.float32)
        normed = (wide_hidden * lax.rsqrt(lax.optimization_barrier(jnp.mean(wide_hidden * wide_hidden, axis=-1, keepdims=True)) + norm_epsilon) * input_norm_scale.astype(jnp.float32)).astype(jnp.bfloat16)
        query_heads = jnp.dot(normed, query_weight, preferred_element_type=jnp.float32).astype(jnp.bfloat16)
        fresh_pairs = jnp.dot(normed, key_value_weight, preferred_element_type=jnp.float32).astype(jnp.bfloat16)
        positions = lengths + decode_step
        rotated_query = rotate(query_heads.astype(jnp.float32).reshape(row_count, QUERY_HEAD_COUNT, HEAD_SIZE), positions).astype(jnp.bfloat16)
        key_new = rotate(fresh_pairs[:, :half_kv].astype(jnp.float32).reshape(row_count, KV_HEADS, HEAD_SIZE), positions).astype(jnp.bfloat16)
        value_new = fresh_pairs[:, half_kv:]
        stored.append(jnp.concatenate([key_new.reshape(row_count, half_kv), value_new], axis=1))
        fresh_keys.append(key_new)
        fresh_values.append(value_new.reshape(row_count, KV_HEADS, HEAD_SIZE))
        key_block = jnp.concatenate([cache_keys, jnp.stack(fresh_keys, axis=1)], axis=1).astype(jnp.float32)
        value_block = jnp.concatenate([cache_values, jnp.stack(fresh_values, axis=1)], axis=1).astype(jnp.float32)
        valid_mask = jnp.concatenate([cache_valid, jnp.ones((row_count, decode_step + 1), dtype=bool)], axis=1)
        grouped = rotated_query.reshape(row_count, KV_HEADS, groups, HEAD_SIZE).astype(jnp.float32)
        scores = jnp.einsum('rkgd,rpkd->rkgp', grouped, key_block) / math.sqrt(HEAD_SIZE)
        scores = jnp.where(valid_mask[:, None, None, :], scores, jnp.float32(-1e+30))
        row_peak = lax.optimization_barrier(jnp.max(scores, axis=-1, keepdims=True))
        weights = jnp.where(valid_mask[:, None, None, :], jnp.exp(scores - row_peak), jnp.float32(0.0))
        softmax_out = (weights / lax.optimization_barrier(jnp.sum(weights, axis=-1, keepdims=True))).astype(jnp.bfloat16)
        attention = jnp.einsum('rkgp,rpkd->rkgd', softmax_out.astype(jnp.float32), value_block).astype(jnp.bfloat16).reshape(row_count, QUERY_HEAD_COUNT * HEAD_SIZE)
        blocked = attention.reshape(BLOCKS, BLOCK, QUERY_HEAD_COUNT * HEAD_SIZE).astype(jnp.float32)
        low_rank = jnp.einsum('bte,bre->btr', blocked, down_matrices).astype(jnp.bfloat16)
        adapted = jnp.einsum('btr,brd->btd', low_rank.astype(jnp.float32), up_matrices).reshape(row_count, MODEL_WIDTH)
        projected = jnp.dot(attention, output_weight, preferred_element_type=jnp.float32)
        hidden = (wide_hidden + projected + adapted).astype(jnp.bfloat16)
    return (hidden, jnp.stack(stored, axis=0))
```

```python
import math

import jax
import jax.numpy as jnp
from jax import lax
from jax.sharding import PartitionSpec as P

MODEL_WIDTH = 8192
HEAD_SIZE = 128
QUERY_HEAD_COUNT = 32
KV_HEADS = 4
BLOCK = 16
STEPS = 2


rope_base = 500000.0
norm_epsilon = 1e-05


def rotate(values_in, positions):
    half_dim = values_in.shape[-1] // 2
    frequency = rope_base ** (
        -(jnp.arange(half_dim, dtype=jnp.float32) * 2.0 / values_in.shape[-1])
    )
    angles = positions.astype(jnp.float32)[:, None, None] * frequency[None, None, :]
    cosine = jnp.cos(angles)
    sine_part = jnp.sin(angles)
    front_half = values_in[..., :half_dim]
    back_half = values_in[..., half_dim:]
    return jnp.concatenate(
        [front_half * cosine - back_half * sine_part, back_half * cosine + front_half * sine_part],
        axis=-1,
    )


def row_adapters(adapter_per_block, adapter_storage_slot, down, up, att_rows):
    tp_count = lax.axis_size("tp")
    own = lax.axis_index("req")
    stored_here = down.shape[0]
    rank = down.shape[1]
    slot = adapter_storage_slot[adapter_per_block]
    other_slot = lax.ppermute(slot, "req", [(0, 1), (1, 0)])

    def piece(which):
        at = jnp.clip(which - own * stored_here, 0, stored_here - 1)
        return jnp.concatenate([jnp.take(down, at, axis=0), jnp.take(up, at, axis=0)], axis=2)

    sent = lax.ppermute(piece(other_slot), "req", [(0, 1), (1, 0)])
    held = jnp.where((slot // stored_here == own)[:, None, None], piece(slot), sent)
    gathered = lax.all_gather(held, "tp", axis=0, tiled=False)
    block = (lax.axis_index("tp") * att_rows) // BLOCK
    mine = lax.dynamic_index_in_dim(gathered, block, axis=1, keepdims=False)
    return mine[:, :, : down.shape[2]], mine[:, :, down.shape[2] :]


def local(
    input_hidden_rows,
    input_norm_scale,
    query_weight,
    key_value_weight,
    output_weight,
    cache,
    lengths,
    adapter_per_block,
    adapter_storage_slot,
    adapter_down_projection,
    adapter_up_projection,
):
    tp_count = lax.axis_size("tp")
    rows_req = input_hidden_rows.shape[0]
    att_rows = cache.shape[0]
    context = cache.shape[1]
    half_kv = cache.shape[2] // 2
    query_width = query_weight.shape[1]
    groups = QUERY_HEAD_COUNT // KV_HEADS
    down_own, up_own = row_adapters(
        adapter_per_block, adapter_storage_slot, adapter_down_projection, adapter_up_projection, att_rows
    )
    cache_keys = cache[:, :, :half_kv].reshape(att_rows, context, KV_HEADS, HEAD_SIZE)
    cache_values = cache[:, :, half_kv:].reshape(att_rows, context, KV_HEADS, HEAD_SIZE)
    cache_valid = jnp.arange(context, dtype=jnp.int32)[None, :] < lengths[:, None]
    scale = input_norm_scale.astype(jnp.float32)

    def norm(wide):
        mean = jnp.mean(wide * wide, axis=-1, keepdims=True)
        return (wide * lax.rsqrt(mean + norm_epsilon) * scale).astype(jnp.bfloat16)

    def exchange(chunks):
        return lax.all_to_all(chunks, "tp", split_axis=0, concat_axis=0, tiled=True)

    def gather_rows(rows):
        spread = exchange(jnp.broadcast_to(rows[None], (tp_count,) + rows.shape))
        return spread.reshape(rows_req, rows.shape[1])

    normed = norm(input_hidden_rows.astype(jnp.float32))
    hidden = lax.dynamic_slice_in_dim(
        input_hidden_rows, lax.axis_index("tp") * att_rows, att_rows, 0
    )
    fresh_keys = []
    fresh_values = []
    stored = []
    for decode_step in range(STEPS):
        query_heads = jnp.dot(normed, query_weight, preferred_element_type=jnp.float32)
        fresh_pairs = jnp.dot(normed, key_value_weight, preferred_element_type=jnp.float32)
        sent = jnp.concatenate([query_heads, fresh_pairs], axis=1).astype(jnp.bfloat16)
        arrived = exchange(sent.reshape(tp_count, att_rows, -1))
        arrived = arrived.transpose(1, 0, 2)
        query_rows = arrived[:, :, :query_width]
        pair_rows = arrived[:, :, query_width:].reshape(att_rows, 2 * half_kv)
        positions = lengths + decode_step
        rotated_query = rotate(
            query_rows.astype(jnp.float32).reshape(att_rows, QUERY_HEAD_COUNT, HEAD_SIZE), positions
        ).astype(jnp.bfloat16)
        key_new = rotate(
            pair_rows[:, :half_kv].astype(jnp.float32).reshape(att_rows, KV_HEADS, HEAD_SIZE),
            positions,
        ).astype(jnp.bfloat16)
        value_new = pair_rows[:, half_kv:]
        stored.append(jnp.concatenate([key_new.reshape(att_rows, half_kv), value_new], axis=1))
        fresh_keys.append(key_new)
        fresh_values.append(value_new.reshape(att_rows, KV_HEADS, HEAD_SIZE))
        key_block = jnp.concatenate([cache_keys, jnp.stack(fresh_keys, axis=1)], axis=1)
        value_block = jnp.concatenate([cache_values, jnp.stack(fresh_values, axis=1)], axis=1)
        valid_mask = jnp.concatenate(
            [cache_valid, jnp.ones((att_rows, decode_step + 1), dtype=bool)], axis=1
        )
        grouped = rotated_query.reshape(att_rows, KV_HEADS, groups, HEAD_SIZE)
        scores = jnp.einsum(
            "rkgd,rpkd->rkgp", grouped, key_block, preferred_element_type=jnp.float32
        ) / math.sqrt(HEAD_SIZE)
        scores = jnp.where(valid_mask[:, None, None, :], scores, jnp.float32(-1e30))
        row_peak = jnp.max(scores, axis=-1, keepdims=True)
        weights = jnp.where(
            valid_mask[:, None, None, :], jnp.exp(scores - row_peak), jnp.float32(0.0)
        )
        softmax_out = (weights / jnp.sum(weights, axis=-1, keepdims=True)).astype(jnp.bfloat16)
        attention = (
            jnp.einsum(
                "rkgp,rpkd->rkgd", softmax_out, value_block, preferred_element_type=jnp.float32
            )
            .astype(jnp.bfloat16)
            .reshape(att_rows, tp_count, query_width)
        )
        head_major = exchange(attention.transpose(1, 0, 2)).reshape(rows_req, query_width)
        low_rank = jnp.einsum(
            "rjk,jdk->rd", attention, down_own, preferred_element_type=jnp.float32
        ).astype(jnp.bfloat16)
        adapted = jnp.einsum(
            "rd,jdc->rjc", low_rank, up_own, preferred_element_type=jnp.float32
        ).reshape(att_rows, MODEL_WIDTH)
        base = hidden.astype(jnp.float32) + adapted
        projected = jnp.dot(head_major, output_weight, preferred_element_type=jnp.float32)
        terms = exchange(projected.reshape(tp_count, att_rows, MODEL_WIDTH))
        hidden = (base + jnp.sum(terms, axis=0)).astype(jnp.bfloat16)
        if decode_step < STEPS - 1:
            normed = gather_rows(norm(hidden.astype(jnp.float32)))
    return (gather_rows(hidden), jnp.stack(stored, axis=0))


def solution(mesh):
    in_specs = (
        P(("parts", "req"), None),
        P(),
        P(None, "tp"),
        P(None, "tp"),
        P("tp", None),
        P(("parts", "req", "tp"), None, None),
        P(("parts", "req", "tp")),
        P(("parts", "req")),
        P(),
        P("req", None, "tp"),
        P("req", None, "tp"),
    )
    out_specs = (P(("parts", "req"), None), P(None, ("parts", "req", "tp"), None))
    return jax.shard_map(local, mesh=mesh, in_specs=in_specs, out_specs=out_specs, check_vma=False)
```

```python
import math

import jax
import jax.numpy as jnp
from jax import lax
from jax.experimental import pallas as pl
from jax.experimental.pallas import tpu as pltpu
from jax.sharding import PartitionSpec as P

MODEL_WIDTH = 8192
HEAD_SIZE = 128
QUERY_HEAD_COUNT = 32
KV_HEADS = 4
BLOCK = 16
STEPS = 2

rope_base = 500000.0
norm_epsilon = 1e-05
term_type = jnp.float32
f32 = jnp.float32
bf16 = jnp.bfloat16
MIB = 1 << 20


def whole(kind=pltpu.VMEM):
    return pl.BlockSpec(memory_space=kind)


def call(body, outs, ins, flops, data_bytes, limit=48):
    return pl.pallas_call(
        body,
        out_shape=outs,
        in_specs=ins,
        out_specs=jax.tree.map(lambda _: whole(), outs),
        compiler_params=pltpu.CompilerParams(vmem_limit_bytes=limit * MIB),
        cost_estimate=pl.CostEstimate(flops=flops, bytes_accessed=data_bytes, transcendentals=0),
    )


def rows_of(ref, start, width):
    pieces = [ref[j, :, pl.ds(start, width)].astype(f32) for j in range(ref.shape[0])]
    return jnp.concatenate(pieces, axis=0).astype(bf16)


def project(source, query_weight, pair_weight, chunk_of, shares):
    depth, query_width = query_weight.shape
    pair_width = pair_weight.shape[1]
    step = 512

    def loop(i, sums):
        at = pl.multiple_of(i * step, step)
        part = chunk_of(at, step)
        rows = pl.ds(at, step)
        return (
            sums[0] + jnp.dot(part, query_weight[rows, :], preferred_element_type=f32),
            sums[1] + jnp.dot(part, pair_weight[rows, :], preferred_element_type=f32),
        )

    count = shares[0] * shares[1]
    zero = (jnp.zeros((count, query_width), f32), jnp.zeros((count, pair_width), f32))
    return lax.fori_loop(0, depth // step, loop, zero, unroll=2)


def store_shares(out, query, pair):
    shares, own, _ = out.shape
    width = query.shape[1]
    for j in range(shares):
        out[j, :, :width] = query[j * own : (j + 1) * own].astype(bf16)
        out[j, :, width:] = pair[j * own : (j + 1) * own].astype(bf16)


def first_projection(hidden, scale, query_weight, pair_weight, own):
    rows, width = hidden.shape
    shares = rows // own

    def body(h, s, wq, wp, out, normed):
        wide = h[...].astype(f32)
        mean = jnp.mean(wide * wide, axis=-1, keepdims=True)
        normed[...] = (wide * lax.rsqrt(mean + norm_epsilon) * s[...].astype(f32)).astype(bf16)
        sums = project(
            h, wq, wp, lambda at, n: normed[:, pl.ds(at, n)], (shares, own)
        )
        store_shares(out, *sums)

    message = query_weight.shape[1] + pair_weight.shape[1]
    return pl.pallas_call(
        body,
        out_shape=jax.ShapeDtypeStruct((shares, own, message), bf16),
        in_specs=[whole()] * 4,
        out_specs=whole(),
        scratch_shapes=[pltpu.VMEM((rows, width), bf16)],
        compiler_params=pltpu.CompilerParams(vmem_limit_bytes=48 * MIB),
        cost_estimate=pl.CostEstimate(
            flops=2 * rows * width * message, bytes_accessed=2 * width * message, transcendentals=0
        ),
    )(hidden, scale, query_weight, pair_weight)


def next_projection(normed, query_weight, pair_weight):
    shares, own, width = normed.shape

    def body(x, wq, wp, out):
        sums = project(x, wq, wp, lambda at, n: rows_of(x, at, n), (shares, own))
        store_shares(out, *sums)

    message = query_weight.shape[1] + pair_weight.shape[1]
    return call(
        body,
        jax.ShapeDtypeStruct((shares, own, message), bf16),
        [whole()] * 3,
        2 * shares * own * width * message,
        2 * width * message,
    )(normed, query_weight, pair_weight)


def attend(arrived, pairs, older, angles, lengths, cache, down, step):
    shares, own, message = arrived.shape
    context, width = cache.shape[1:]
    half = width // 2
    query_width = QUERY_HEAD_COUNT * HEAD_SIZE // shares
    per_share = query_width // HEAD_SIZE
    groups = QUERY_HEAD_COUNT // KV_HEADS
    pair_inside = pairs is None
    rank = down.shape[1]

    def body(*refs):
        refs = list(refs)
        lens, x = refs.pop(0), refs.pop(0)
        pair_ref = None if pair_inside else refs.pop(0)
        old = refs.pop(0) if step else None
        cos_ref, sin_ref, kv, down_ref, out, new = refs
        place = lax.broadcasted_iota(jnp.int32, (groups, context), 1)
        rows = [x[j].astype(f32) for j in range(shares)]
        outputs = []
        fresh = []
        for r in range(own):
            cosine = cos_ref[r : r + 1, :]
            sine = sin_ref[r : r + 1, :]

            def turn(v):
                return v * cosine + pltpu.roll(v, HEAD_SIZE // 2, 1) * sine

            def pair_head(c):
                if pair_inside:
                    return rows[c][r : r + 1, query_width:]
                return pair_ref[r : r + 1, c * HEAD_SIZE : (c + 1) * HEAD_SIZE].astype(f32)

            heads = []
            line = []
            for g in range(KV_HEADS):
                line.append(turn(pair_head(g)).astype(bf16))
            for g in range(KV_HEADS):
                line.append(pair_head(KV_HEADS + g).astype(bf16))
            fresh.append(jnp.concatenate([v.astype(f32) for v in line], axis=1))
            for g in range(KV_HEADS):
                column = slice(g * HEAD_SIZE, (g + 1) * HEAD_SIZE)
                value_column = slice(half + g * HEAD_SIZE, half + (g + 1) * HEAD_SIZE)
                lines = []
                for h in range(g * groups, (g + 1) * groups):
                    at = (h % per_share) * HEAD_SIZE
                    lines.append(rows[h // per_share][r : r + 1, at : at + HEAD_SIZE])
                query = turn(jnp.concatenate(lines, axis=0)).astype(bf16)
                scores = lax.dot_general(
                    query, kv[r, :, column], (((1,), (1,)), ((), ())), preferred_element_type=f32
                ) * (1.0 / math.sqrt(HEAD_SIZE))
                scores = jnp.where(place < lens[r], scores, f32(-1e30))
                new_keys = [line[g].astype(f32)]
                new_values = [line[KV_HEADS + g].astype(f32)]
                if step:
                    new_keys.append(old[r : r + 1, column].astype(f32))
                    new_values.append(old[r : r + 1, value_column].astype(f32))
                wide_query = query.astype(f32)
                extra = [
                    jnp.sum(wide_query * k, axis=1, keepdims=True) * (1.0 / math.sqrt(HEAD_SIZE))
                    for k in new_keys
                ]
                peak = jnp.max(scores, axis=1, keepdims=True)
                for e in extra:
                    peak = jnp.maximum(peak, e)
                weight = jnp.exp(scores - peak)
                extra = [jnp.exp(e - peak) for e in extra]
                total = jnp.sum(weight, axis=1, keepdims=True)
                for e in extra:
                    total = total + e
                result = jnp.dot(
                    (weight / total).astype(bf16), kv[r, :, value_column], preferred_element_type=f32
                )
                for e, v in zip(extra, new_values):
                    result = result + (e / total).astype(bf16).astype(f32) * v
                heads.append(result)
            outputs.append(heads)
        new[...] = jnp.concatenate(fresh, axis=0).astype(bf16)
        low = jnp.zeros((own, rank), f32)
        for j in range(shares):
            lines = []
            for r in range(own):
                cells = []
                for h in range(j * per_share, (j + 1) * per_share):
                    at = h % groups
                    cells.append(outputs[r][h // groups][at : at + 1, :])
                lines.append(jnp.concatenate(cells, axis=1))
            share = jnp.concatenate(lines, axis=0).astype(bf16)
            out[j, :, :query_width] = share
            low = low + lax.dot_general(
                share, down_ref[j], (((1,), (1,)), ((), ())), preferred_element_type=f32
            )
        padded = jnp.concatenate([low, jnp.zeros((own, HEAD_SIZE - rank), f32)], axis=1).astype(bf16)
        for j in range(shares):
            out[j, :, query_width:] = padded

    operands = [lengths, arrived]
    specs = [whole(pltpu.SMEM), whole()]
    for extra in ([] if pair_inside else [pairs]) + ([older] if step else []):
        operands.append(extra)
        specs.append(whole())
    operands += [angles[0], angles[1], cache, down]
    specs += [whole()] * 4
    return call(
        body,
        (
            jax.ShapeDtypeStruct((shares, own, query_width + HEAD_SIZE), bf16),
            jax.ShapeDtypeStruct((own, width), bf16),
        ),
        specs,
        8 * own * QUERY_HEAD_COUNT * HEAD_SIZE * context,
        2 * own * context * width,
    )(*operands)


def output_terms(arrived, output_weight, up, blocks):
    shares, own, _ = arrived.shape
    query_width, width = output_weight.shape
    share_width = up.shape[2]
    rank = up.shape[1]
    rows = shares * own
    step = 1024

    def body(mine, x, wo, up_ref, out, total):
        heads = rows_of(x, 0, query_width)
        low = rows_of(x, query_width, HEAD_SIZE)[:, :rank]

        def loop(i, carry):
            at = pl.multiple_of(i * step, step)
            total[:, pl.ds(at, step)] = jnp.dot(
                heads, wo[:, pl.ds(at, step)], preferred_element_type=f32
            )
            return carry

        lax.fori_loop(0, width // step, loop, 0)
        start = pl.multiple_of(mine[0] * share_width, share_width)
        for b in range(blocks):
            lines = slice(b * BLOCK, (b + 1) * BLOCK)
            total[lines, pl.ds(start, share_width)] += jnp.dot(
                low[lines], up_ref[b], preferred_element_type=f32
            )
        for j in range(shares):
            out[j] = total[j * own : (j + 1) * own, :].astype(out.dtype)

    return pl.pallas_call(
        body,
        out_shape=jax.ShapeDtypeStruct((shares, own, width), term_type),
        in_specs=[whole(pltpu.SMEM)] + [whole()] * 3,
        out_specs=whole(),
        scratch_shapes=[pltpu.VMEM((rows, width), f32)],
        compiler_params=pltpu.CompilerParams(vmem_limit_bytes=48 * MIB),
        cost_estimate=pl.CostEstimate(
            flops=2 * rows * width * query_width,
            bytes_accessed=2 * width * query_width,
            transcendentals=0,
        ),
    )(lax.axis_index("tp").astype(jnp.int32).reshape(1), arrived, output_weight, up)


def close_step(terms, hidden, scale):
    shares, own, width = terms.shape
    normed = scale is not None

    def body(t, h, *refs):
        total = h[...].astype(f32)
        for j in range(shares):
            total = total + t[j].astype(f32)
        rounded = total.astype(bf16)
        spread = rounded
        if normed:
            s, out, kept = refs
            kept[...] = rounded
            wide = rounded.astype(f32)
            mean = jnp.mean(wide * wide, axis=-1, keepdims=True)
            spread = (wide * lax.rsqrt(mean + norm_epsilon) * s[...].astype(f32)).astype(bf16)
        else:
            (out,) = refs
        for j in range(shares):
            out[j] = spread

    outs = [jax.ShapeDtypeStruct((shares, own, width), bf16)]
    operands = [terms, hidden]
    if normed:
        outs.append(jax.ShapeDtypeStruct((own, width), bf16))
        operands.append(scale)
    return call(
        body, tuple(outs), [whole()] * len(operands), 8 * own * width, 6 * shares * own * width
    )(*operands)


def block_adapters(adapter_per_block, adapter_storage_slot, down, up):
    own = lax.axis_index("req")
    stored_here = down.shape[0]
    slot = adapter_storage_slot[adapter_per_block]
    other_slot = lax.ppermute(slot, "req", [(0, 1), (1, 0)])

    def piece(which):
        at = jnp.clip(which - own * stored_here, 0, stored_here - 1)
        return jnp.concatenate([jnp.take(down, at, axis=0), jnp.take(up, at, axis=0)], axis=2)

    sent = lax.ppermute(piece(other_slot), "req", [(0, 1), (1, 0)])
    held = jnp.where((slot // stored_here == own)[:, None, None], piece(slot), sent)
    return held[:, :, : down.shape[2]], held[:, :, down.shape[2] :]


def exchange(chunks):
    return lax.all_to_all(chunks, "tp", split_axis=0, concat_axis=0, tiled=True)


def local(
    input_hidden_rows,
    input_norm_scale,
    query_weight,
    key_value_weight,
    output_weight,
    cache,
    lengths,
    adapter_per_block,
    adapter_storage_slot,
    adapter_down_projection,
    adapter_up_projection,
):
    tp_count = lax.axis_size("tp")
    tp_index = lax.axis_index("tp")
    rows_req = input_hidden_rows.shape[0]
    own = cache.shape[0]
    blocks = rows_req // BLOCK
    width = input_hidden_rows.shape[1]
    query_width = query_weight.shape[1]
    scale = input_norm_scale.reshape(1, width)
    down, up = block_adapters(
        adapter_per_block, adapter_storage_slot, adapter_down_projection, adapter_up_projection
    )
    down_chunks = jnp.repeat(down, tp_count // blocks, axis=0)
    down_own = exchange(down_chunks)
    half_head = HEAD_SIZE // 2
    frequency = rope_base ** (-(jnp.arange(half_head, dtype=f32) * 2.0 / HEAD_SIZE))
    hidden = lax.dynamic_slice_in_dim(input_hidden_rows, tp_index * own, own, 0)
    stored = []
    message = first_projection(input_hidden_rows, scale, query_weight, key_value_weight, own)
    for step in range(STEPS):
        angle = (lengths + step).astype(f32)[:, None] * frequency[None, :]
        cosine, sine = jnp.cos(angle), jnp.sin(angle)
        angles = (
            jnp.concatenate([cosine, cosine], axis=1),
            jnp.concatenate([-sine, sine], axis=1),
        )
        arrived = exchange(message)
        pairs = None
        if key_value_weight.shape[1] != HEAD_SIZE:
            pairs = arrived[:, :, query_width:].transpose(1, 0, 2).reshape(own, -1)
        attended, fresh = attend(
            arrived, pairs, stored[-1] if step else None, angles, lengths, cache, down_own, step
        )
        stored.append(fresh)
        terms = exchange(output_terms(exchange(attended), output_weight, up, blocks))
        if step < STEPS - 1:
            spread, hidden = close_step(terms, hidden, scale)
            message = next_projection(exchange(spread), query_weight, key_value_weight)
        else:
            (spread,) = close_step(terms, hidden, None)
    return (exchange(spread).reshape(rows_req, width), jnp.stack(stored, axis=0))


def solution(mesh):
    in_specs = (
        P(("parts", "req"), None),
        P(),
        P(None, "tp"),
        P(None, "tp"),
        P("tp", None),
        P(("parts", "req", "tp"), None, None),
        P(("parts", "req", "tp")),
        P(("parts", "req")),
        P(),
        P("req", None, "tp"),
        P("req", None, "tp"),
    )
    out_specs = (P(("parts", "req"), None), P(None, ("parts", "req", "tp"), None))
    return jax.shard_map(local, mesh=mesh, in_specs=in_specs, out_specs=out_specs, check_vma=False)
```

```python
import math

import jax
import jax.numpy as jnp
from jax import lax
from jax.experimental import pallas as pl
from jax.experimental.pallas import tpu as pltpu
from jax.sharding import PartitionSpec as P

MODEL_WIDTH = 8192
HEAD_SIZE = 128
QUERY_HEAD_COUNT = 32
KV_HEADS = 4
BLOCK = 16
STEPS = 2

rope_base = 500000.0
norm_epsilon = 1e-05
term_type = jnp.bfloat16
f32 = jnp.float32
bf16 = jnp.bfloat16
MIB = 1 << 20


def whole(kind=pltpu.VMEM):
    return pl.BlockSpec(memory_space=kind)


def call(body, outs, ins, flops, data_bytes, limit=16):
    return pl.pallas_call(
        body,
        out_shape=outs,
        in_specs=ins,
        out_specs=jax.tree.map(lambda _: whole(), outs),
        compiler_params=pltpu.CompilerParams(vmem_limit_bytes=limit * MIB),
        cost_estimate=pl.CostEstimate(flops=flops, bytes_accessed=data_bytes, transcendentals=0),
    )


def far(array):
    return pltpu.with_memory_space_constraint(array, pltpu.HBM)


def rows_of(ref, start, width):
    pieces = [ref[j, :, pl.ds(start, width)].astype(f32) for j in range(ref.shape[0])]
    return jnp.concatenate(pieces, axis=0).astype(bf16)


def streamed(weights, kept, sems, step, axis):
    def copies(i):
        piece = pl.ds(pl.multiple_of(i * step, step), step)
        at = (piece, slice(None)) if axis == 0 else (slice(None), piece)
        return [
            pltpu.make_async_copy(w.at[at], k.at[at], sems.at[n, i])
            for n, (w, k) in enumerate(zip(weights, kept))
        ]

    return copies


def project(weights, chunk_of, rows, step, copies):
    depth = weights[0].shape[0]

    def loop(i, sums):
        at = pl.multiple_of(i * step, step)
        for copy in copies(i):
            copy.wait()
        part = chunk_of(at, step)
        return tuple(
            total + jnp.dot(part, w[pl.ds(at, step), :], preferred_element_type=f32)
            for total, w in zip(sums, weights)
        )

    zero = tuple(jnp.zeros((rows, w.shape[1]), f32) for w in weights)
    return lax.fori_loop(0, depth // step, loop, zero)


def store_shares(out, query, pair):
    shares, own, _ = out.shape
    width = query.shape[1]
    for j in range(shares):
        lines = slice(j * own, (j + 1) * own)
        out[j, :, :width] = query[lines].astype(bf16)
        out[j, :, width:] = pair[lines].astype(bf16)


def projection(source, weights, own, scale=None):
    width = weights[0].shape[0]
    shares = lax.axis_size("tp")
    rows = shares * own
    message = sum(w.shape[1] for w in weights)
    step = 1024
    parts = width // step
    first = scale is not None

    def body(*refs):
        if first:
            source_ref, s, wq, wp, out, kept_q, kept_p, sems, x, gains, normed, pre = refs
            loads = [
                pltpu.make_async_copy(source_ref, x, pre.at[0]),
                pltpu.make_async_copy(s, gains, pre.at[1]),
            ]
            for load in loads:
                load.start()
        else:
            x, wq, wp, out, kept_q, kept_p, sems = refs
        copies = streamed((wq, wp), (kept_q, kept_p), sems, step, 0)
        for i in range(parts):
            for copy in copies(i):
                copy.start()
        if first:
            for load in loads:
                load.wait()
            wide = x[...].astype(f32)
            ratio = lax.rsqrt(jnp.mean(wide * wide, axis=-1, keepdims=True) + norm_epsilon)
            gain = gains[...].astype(f32)
            for c in range(width // HEAD_SIZE):
                columns = slice(c * HEAD_SIZE, (c + 1) * HEAD_SIZE)
                normed[:, columns] = (
                    x[:, columns].astype(f32) * ratio * gain[c : c + 1, :]
                ).astype(bf16)
            chunk_of = lambda at, n: normed[:, pl.ds(at, n)]
        else:
            chunk_of = lambda at, n: rows_of(x, at, n)
        sums = project((kept_q, kept_p), chunk_of, rows, step, copies)
        store_shares(out, *sums)

    scratch = [pltpu.VMEM(w.shape, bf16) for w in weights]
    scratch.append(pltpu.SemaphoreType.DMA((2, parts)))
    operands = [source, *map(far, weights)]
    specs = [whole(), whole(pltpu.HBM), whole(pltpu.HBM)]
    if first:
        operands[:1] = [far(source), far(scale)]
        specs[:1] = [whole(pltpu.HBM)] * 2
        scratch += [
            pltpu.VMEM(source.shape, bf16),
            pltpu.VMEM(scale.shape, bf16),
            pltpu.VMEM(source.shape, bf16),
            pltpu.SemaphoreType.DMA((2,)),
        ]
    return pl.pallas_call(
        body,
        out_shape=jax.ShapeDtypeStruct((shares, own, message), bf16),
        in_specs=specs,
        out_specs=whole(),
        scratch_shapes=scratch,
        compiler_params=pltpu.CompilerParams(vmem_limit_bytes=24 * MIB),
        cost_estimate=pl.CostEstimate(
            flops=2 * rows * width * message,
            bytes_accessed=2 * width * message,
            transcendentals=0,
        ),
    )(*operands)


def fetch(block, per_block, slots, side, here, other, target, sem):
    stored_here = here.shape[0]
    slot = slots[per_block[block]]
    at = lax.rem(slot, jnp.int32(stored_here))
    mine = lax.div(slot, jnp.int32(stored_here)) == side[0]

    @pl.when(mine)
    def _():
        pltpu.make_async_copy(here.at[at], target.at[block], sem.at[block]).start()

    @pl.when(jnp.logical_not(mine))
    def _():
        pltpu.make_async_copy(other.at[at], target.at[block], sem.at[block]).start()

    return pltpu.make_async_copy(here.at[0], target.at[block], sem.at[block])


def add_down(message, adapters, here, other, blocks):
    shares, own, width = message.shape
    rank, columns = here.shape[1:]
    lead = rank // own * columns

    def body(per_block, slots, side, m, here_ref, other_ref, out, piece, sem):
        waits = [
            fetch(b, per_block, slots, side, here_ref, other_ref, piece, sem)
            for b in range(blocks)
        ]
        for j in range(shares):
            out[j, :, lead:] = m[j]
        for wait in waits:
            wait.wait()
        for b in range(blocks):
            lines = [
                piece[b, m * own : (m + 1) * own, :].astype(f32) for m in range(rank // own)
            ]
            packed = jnp.concatenate(lines, axis=1).astype(bf16)
            for j in range(b * BLOCK // own, (b + 1) * BLOCK // own):
                out[j, :, :lead] = packed

    smem = whole(pltpu.SMEM)
    return pl.pallas_call(
        body,
        out_shape=jax.ShapeDtypeStruct((shares, own, lead + width), bf16),
        in_specs=[smem, smem, smem, whole(), whole(pltpu.HBM), whole(pltpu.HBM)],
        out_specs=whole(),
        scratch_shapes=[
            pltpu.VMEM((blocks, rank, columns), bf16),
            pltpu.SemaphoreType.DMA((blocks,)),
        ],
        compiler_params=pltpu.CompilerParams(vmem_limit_bytes=16 * MIB),
    )(*adapters, message, far(here), far(other))


def attend(arrived, pairs, older, angles, lengths, cache, down, step, lead, rank):
    shares, own, message = arrived.shape
    context, width = cache.shape[1:]
    half = width // 2
    query_width = QUERY_HEAD_COUNT * HEAD_SIZE // shares
    per_share = query_width // HEAD_SIZE
    groups = QUERY_HEAD_COUNT // KV_HEADS
    pair_inside = pairs is None

    def body(*refs):
        refs = list(refs)
        lens, x = refs.pop(0), refs.pop(0)
        pair_ref = None if pair_inside else refs.pop(0)
        old = refs.pop(0) if step else None
        cos_ref, sin_ref, kv = refs[:3]
        if step:
            down_ref, out, new = refs[3:]
        else:
            out, new, down_ref = refs[3:]
            for j in range(shares):
                lines = [
                    x[j, :, m * query_width : (m + 1) * query_width].astype(f32)
                    for m in range(rank // own)
                ]
                down_ref[j] = jnp.concatenate(lines, axis=0).astype(bf16)
        place = lax.broadcasted_iota(jnp.int32, (groups, context), 1)
        rows = [x[j, :, lead:].astype(f32) for j in range(shares)]
        outputs = []
        fresh = []
        for r in range(own):
            cosine = cos_ref[r : r + 1, :]
            sine = sin_ref[r : r + 1, :]

            def turn(v):
                return v * cosine + pltpu.roll(v, HEAD_SIZE // 2, 1) * sine

            def pair_head(c):
                if pair_inside:
                    return rows[c][r : r + 1, query_width:]
                return pair_ref[r : r + 1, c * HEAD_SIZE : (c + 1) * HEAD_SIZE].astype(f32)

            heads = []
            line = []
            for g in range(KV_HEADS):
                line.append(turn(pair_head(g)).astype(bf16))
            for g in range(KV_HEADS):
                line.append(pair_head(KV_HEADS + g).astype(bf16))
            fresh.append(jnp.concatenate([v.astype(f32) for v in line], axis=1))
            for g in range(KV_HEADS):
                column = slice(g * HEAD_SIZE, (g + 1) * HEAD_SIZE)
                value_column = slice(half + g * HEAD_SIZE, half + (g + 1) * HEAD_SIZE)
                lines = []
                for h in range(g * groups, (g + 1) * groups):
                    at = (h % per_share) * HEAD_SIZE
                    lines.append(rows[h // per_share][r : r + 1, at : at + HEAD_SIZE])
                query = turn(jnp.concatenate(lines, axis=0)).astype(bf16)
                scores = lax.dot_general(
                    query, kv[r, :, column], (((1,), (1,)), ((), ())), preferred_element_type=f32
                ) * (1.0 / math.sqrt(HEAD_SIZE))
                scores = jnp.where(place < lens[r], scores, f32(-1e30))
                new_keys = [line[g].astype(f32)]
                new_values = [line[KV_HEADS + g].astype(f32)]
                if step:
                    new_keys.append(old[r : r + 1, column].astype(f32))
                    new_values.append(old[r : r + 1, value_column].astype(f32))
                wide_query = query.astype(f32)
                extra = [
                    jnp.sum(wide_query * k, axis=1, keepdims=True) * (1.0 / math.sqrt(HEAD_SIZE))
                    for k in new_keys
                ]
                peak = jnp.max(scores, axis=1, keepdims=True)
                for e in extra:
                    peak = jnp.maximum(peak, e)
                weight = jnp.exp(scores - peak)
                extra = [jnp.exp(e - peak) for e in extra]
                total = jnp.sum(weight, axis=1, keepdims=True)
                for e in extra:
                    total = total + e
                result = jnp.dot(
                    (weight / total).astype(bf16), kv[r, :, value_column], preferred_element_type=f32
                )
                for e, v in zip(extra, new_values):
                    result = result + (e / total).astype(bf16).astype(f32) * v
                heads.append(result)
            outputs.append(heads)
        new[...] = jnp.concatenate(fresh, axis=0).astype(bf16)
        low = jnp.zeros((own, rank), f32)
        for j in range(shares):
            lines = []
            for r in range(own):
                cells = []
                for h in range(j * per_share, (j + 1) * per_share):
                    at = h % groups
                    cells.append(outputs[r][h // groups][at : at + 1, :])
                lines.append(jnp.concatenate(cells, axis=1))
            share = jnp.concatenate(lines, axis=0).astype(bf16)
            out[j, :, :query_width] = share
            low = low + lax.dot_general(
                share, down_ref[j], (((1,), (1,)), ((), ())), preferred_element_type=f32
            )
        padded = jnp.concatenate([low, jnp.zeros((own, HEAD_SIZE - rank), f32)], axis=1).astype(bf16)
        for j in range(shares):
            out[j, :, query_width:] = padded

    operands = [lengths, arrived]
    specs = [whole(pltpu.SMEM), whole()]
    for extra in ([] if pair_inside else [pairs]) + ([older] if step else []):
        operands.append(extra)
        specs.append(whole())
    operands += [angles[0], angles[1], cache] + ([down] if step else [])
    specs += [whole()] * (4 if step else 3)
    outs = [
        jax.ShapeDtypeStruct((shares, own, query_width + HEAD_SIZE), bf16),
        jax.ShapeDtypeStruct((own, width), bf16),
    ]
    if not step:
        outs.append(jax.ShapeDtypeStruct((shares, rank, query_width), bf16))
    return pl.pallas_call(
        body,
        out_shape=tuple(outs),
        in_specs=specs,
        out_specs=(whole(),) * len(outs),
        compiler_params=pltpu.CompilerParams(vmem_limit_bytes=16 * MIB),
        cost_estimate=pl.CostEstimate(
            flops=8 * own * QUERY_HEAD_COUNT * HEAD_SIZE * context,
            bytes_accessed=2 * own * context * width,
            transcendentals=0,
        ),
    )(*operands)


def output_terms(arrived, output_weight, adapters, here, other, blocks):
    shares, own, _ = arrived.shape
    query_width, width = output_weight.shape
    rank, share_width = here.shape[1:]
    rows = shares * own
    step = 1024
    parts = width // step

    def body(mine, per_block, slots, side, x, wo, here_ref, other_ref, *refs):
        out, total, kept, up, sem, sems = refs
        copies = streamed((wo,), (kept,), sems, step, 1)
        for i in range(parts):
            copies(i)[0].start()
        waits = [
            fetch(b, per_block, slots, side, here_ref, other_ref, up, sem) for b in range(blocks)
        ]
        heads = rows_of(x, 0, query_width)
        low = rows_of(x, query_width, HEAD_SIZE)[:, :rank]

        def loop(i, carry):
            at = pl.multiple_of(i * step, step)
            copies(i)[0].wait()
            total[:, pl.ds(at, step)] = jnp.dot(
                heads, kept[:, pl.ds(at, step)], preferred_element_type=f32
            )
            return carry

        lax.fori_loop(0, parts, loop, 0)
        start = pl.multiple_of(mine[0] * share_width, share_width)
        for b in range(blocks):
            waits[b].wait()
            lines = slice(b * BLOCK, (b + 1) * BLOCK)
            total[lines, pl.ds(start, share_width)] += jnp.dot(
                low[lines], up[b], preferred_element_type=f32
            )
        for j in range(shares):
            out[j] = total[j * own : (j + 1) * own, :].astype(out.dtype)

    smem, hbm = whole(pltpu.SMEM), whole(pltpu.HBM)
    return pl.pallas_call(
        body,
        out_shape=jax.ShapeDtypeStruct((shares, own, width), term_type),
        in_specs=[smem] * 4 + [whole(), hbm, hbm, hbm],
        out_specs=whole(),
        scratch_shapes=[
            pltpu.VMEM((rows, width), f32),
            pltpu.VMEM(output_weight.shape, bf16),
            pltpu.VMEM((blocks, rank, share_width), bf16),
            pltpu.SemaphoreType.DMA((blocks,)),
            pltpu.SemaphoreType.DMA((1, parts)),
        ],
        compiler_params=pltpu.CompilerParams(vmem_limit_bytes=24 * MIB),
        cost_estimate=pl.CostEstimate(
            flops=2 * rows * width * query_width,
            bytes_accessed=2 * width * query_width,
            transcendentals=0,
        ),
    )(
        lax.axis_index("tp").astype(jnp.int32).reshape(1),
        *adapters,
        arrived,
        far(output_weight),
        far(here),
        far(other),
    )


def close_step(terms, hidden, scale):
    shares, own, width = terms.shape
    normed = scale is not None

    def body(t, h, *refs):
        total = h[...].astype(f32)
        for j in range(shares):
            total = total + t[j].astype(f32)
        rounded = total.astype(bf16)
        spread = rounded
        if normed:
            s, out, kept = refs
            kept[...] = rounded
            wide = rounded.astype(f32)
            mean = jnp.mean(wide * wide, axis=-1, keepdims=True)
            wide = wide * lax.rsqrt(mean + norm_epsilon)
            gain = s[...].astype(f32)
            spread = jnp.concatenate(
                [
                    wide[:, c * HEAD_SIZE : (c + 1) * HEAD_SIZE] * gain[c : c + 1, :]
                    for c in range(width // HEAD_SIZE)
                ],
                axis=1,
            ).astype(bf16)
        else:
            (out,) = refs
        for j in range(shares):
            out[j] = spread

    outs = [jax.ShapeDtypeStruct((shares, own, width), bf16)]
    operands = [terms, hidden]
    if normed:
        outs.append(jax.ShapeDtypeStruct((own, width), bf16))
        operands.append(scale)
    return call(
        body, tuple(outs), [whole()] * len(operands), 8 * own * width, 6 * shares * own * width
    )(*operands)


def exchange(chunks):
    return lax.all_to_all(chunks, "tp", split_axis=0, concat_axis=0, tiled=True)


def local(
    input_hidden_rows,
    input_norm_scale,
    query_weight,
    key_value_weight,
    output_weight,
    cache,
    lengths,
    adapter_per_block,
    adapter_storage_slot,
    adapter_down_projection,
    adapter_up_projection,
):
    tp_count = lax.axis_size("tp")
    tp_index = lax.axis_index("tp")
    rows_req = input_hidden_rows.shape[0]
    own = cache.shape[0]
    blocks = rows_req // BLOCK
    width = input_hidden_rows.shape[1]
    query_width = query_weight.shape[1]
    rank = adapter_down_projection.shape[1]
    scale = input_norm_scale.reshape(width // HEAD_SIZE, HEAD_SIZE)
    adapters = (
        adapter_per_block,
        adapter_storage_slot,
        lax.axis_index("req").astype(jnp.int32).reshape(1),
    )
    cores = [(0, 1), (1, 0)]
    other_down = lax.ppermute(adapter_down_projection, "req", cores)
    other_up = lax.ppermute(adapter_up_projection, "req", cores)
    lead = rank // own * query_width
    half_head = HEAD_SIZE // 2
    frequency = rope_base ** (-(jnp.arange(half_head, dtype=f32) * 2.0 / HEAD_SIZE))
    hidden = lax.dynamic_slice_in_dim(input_hidden_rows, tp_index * own, own, 0)
    stored = []
    weights = (query_weight, key_value_weight)
    message = projection(input_hidden_rows, weights, own, scale)
    message = add_down(message, adapters, adapter_down_projection, other_down, blocks)
    down = None
    for step in range(STEPS):
        angle = (lengths + step).astype(f32)[:, None] * frequency[None, :]
        cosine, sine = jnp.cos(angle), jnp.sin(angle)
        angles = (
            jnp.concatenate([cosine, cosine], axis=1),
            jnp.concatenate([-sine, sine], axis=1),
        )
        arrived = exchange(message)
        start = 0 if step else lead
        pairs = None
        if key_value_weight.shape[1] != HEAD_SIZE:
            pairs = arrived[:, :, start + query_width :].transpose(1, 0, 2).reshape(own, -1)
        attended, fresh, *first = attend(
            arrived,
            pairs,
            stored[-1] if step else None,
            angles,
            lengths,
            cache,
            down,
            step,
            start,
            rank,
        )
        stored.append(fresh)
        if not step:
            (down,) = first
        terms = exchange(
            output_terms(
                exchange(attended), output_weight, adapters, adapter_up_projection, other_up, blocks
            )
        )
        if step < STEPS - 1:
            spread, hidden = close_step(terms, hidden, scale)
            message = projection(exchange(spread), weights, own)
        else:
            (spread,) = close_step(terms, hidden, None)
    return (exchange(spread).reshape(rows_req, width), jnp.stack(stored, axis=0))


def solution(mesh):
    in_specs = (
        P(("parts", "req"), None),
        P(),
        P(None, "tp"),
        P(None, "tp"),
        P("tp", None),
        P(("parts", "req", "tp"), None, None),
        P(("parts", "req", "tp")),
        P(("parts", "req")),
        P(),
        P("req", None, "tp"),
        P("req", None, "tp"),
    )
    out_specs = (P(("parts", "req"), None), P(None, ("parts", "req", "tp"), None))
    return jax.shard_map(local, mesh=mesh, in_specs=in_specs, out_specs=out_specs, check_vma=False)
```

```python
import math

import jax
import jax.numpy as jnp
from jax import lax
from jax.experimental import pallas as pl
from jax.experimental.pallas import tpu as pltpu
from jax.sharding import PartitionSpec as P

MODEL_WIDTH = 8192
HEAD_SIZE = 128
QUERY_HEAD_COUNT = 32
KV_HEADS = 4
BLOCK = 16
STEPS = 2

rope_base = 500000.0
norm_epsilon = 1e-05
term_type = jnp.bfloat16
f32 = jnp.float32
bf16 = jnp.bfloat16
MIB = 1 << 20


def whole(kind=pltpu.VMEM):
    return pl.BlockSpec(memory_space=kind)


def call(body, outs, ins, flops, data_bytes, limit=16):
    return pl.pallas_call(
        body,
        out_shape=outs,
        in_specs=ins,
        out_specs=jax.tree.map(lambda _: whole(), outs),
        compiler_params=pltpu.CompilerParams(vmem_limit_bytes=limit * MIB),
        cost_estimate=pl.CostEstimate(flops=flops, bytes_accessed=data_bytes, transcendentals=0),
    )


def far(array):
    return pltpu.with_memory_space_constraint(array, pltpu.HBM)


def rows_of(ref, start, width):
    pieces = [ref[j, :, pl.ds(start, width)].astype(f32) for j in range(ref.shape[0])]
    return jnp.concatenate(pieces, axis=0).astype(bf16)


def streamed(weights, kept, sems, step, axis):
    def copies(i):
        piece = pl.ds(pl.multiple_of(i * step, step), step)
        at = (piece, slice(None)) if axis == 0 else (slice(None), piece)
        return [
            pltpu.make_async_copy(w.at[at], k.at[at], sems.at[n, i])
            for n, (w, k) in enumerate(zip(weights, kept))
        ]

    return copies


def project(weights, chunk_of, rows, step, copies=None):
    depth = weights[0].shape[0]
    sums = [jnp.zeros((rows, w.shape[1]), f32) for w in weights]
    for i in range(depth // step):
        at = i * step
        if copies is not None:
            for copy in copies(i):
                copy.wait()
        part = chunk_of(at, step)
        sums = [
            total + jnp.dot(part, w[at : at + step, :], preferred_element_type=f32)
            for total, w in zip(sums, weights)
        ]
    return sums


def store_shares(out, query, pair):
    shares, own, _ = out.shape
    width = query.shape[1]
    for j in range(shares):
        lines = slice(j * own, (j + 1) * own)
        out[j, :, :width] = query[lines].astype(bf16)
        out[j, :, width:] = pair[lines].astype(bf16)


def cost(flops, data_bytes):
    return pl.CostEstimate(flops=flops, bytes_accessed=data_bytes, transcendentals=0)


def first_projection(source, scale, weights, own):
    rows, width = source.shape
    shares = rows // own
    message = sum(w.shape[1] for w in weights)
    step = 1024
    parts = width // step

    def body(mine, source_ref, s, wq, wp, out, held, kept_q, kept_p, sems, x, gains, wide, normed, pre):
        loads = [
            pltpu.make_async_copy(source_ref, x, pre.at[0]),
            pltpu.make_async_copy(s, gains, pre.at[1]),
        ]
        for load in loads:
            load.start()
        copies = streamed((wq, wp), (kept_q, kept_p), sems, step, 0)
        for i in range(parts):
            for copy in copies(i):
                copy.start()
        for load in loads:
            load.wait()
        wide[...] = x[...].astype(f32)
        lines = wide[:own, :]
        for j in range(1, shares):
            lines = jnp.where(mine[0] == j, wide[j * own : (j + 1) * own, :], lines)
        held[...] = lines.astype(bf16)
        value = wide[...]
        ratio = lax.rsqrt(jnp.mean(value * value, axis=-1, keepdims=True) + norm_epsilon)
        gain = gains[...].astype(f32)
        for c in range(width // HEAD_SIZE):
            columns = slice(c * HEAD_SIZE, (c + 1) * HEAD_SIZE)
            normed[:, columns] = (wide[:, columns] * ratio * gain[c : c + 1, :]).astype(bf16)
        sums = project(
            (kept_q, kept_p), lambda at, n: normed[:, at : at + n], rows, step, copies
        )
        store_shares(out, *sums)

    return pl.pallas_call(
        body,
        out_shape=(
            jax.ShapeDtypeStruct((shares, own, message), bf16),
            jax.ShapeDtypeStruct((own, width), bf16),
        ),
        in_specs=[whole(pltpu.SMEM)] + [whole(pltpu.HBM)] * 4,
        out_specs=(whole(), whole()),
        scratch_shapes=[pltpu.VMEM(w.shape, bf16) for w in weights]
        + [
            pltpu.SemaphoreType.DMA((2, parts)),
            pltpu.VMEM(source.shape, bf16),
            pltpu.VMEM(scale.shape, bf16),
            pltpu.VMEM(source.shape, f32),
            pltpu.VMEM(source.shape, bf16),
            pltpu.SemaphoreType.DMA((2,)),
        ],
        compiler_params=pltpu.CompilerParams(vmem_limit_bytes=24 * MIB),
        cost_estimate=cost(2 * rows * width * message, 2 * width * message),
    )(own_index("tp"), far(source), far(scale), *map(far, weights))


def next_projection(normed, weights):
    shares, own, width = normed.shape
    message = sum(w.shape[1] for w in weights)

    def body(x, wq, wp, out):
        store_shares(out, *project((wq, wp), lambda at, n: rows_of(x, at, n), shares * own, 1024))

    return call(
        body,
        jax.ShapeDtypeStruct((shares, own, message), bf16),
        [whole()] * 3,
        2 * shares * own * width * message,
        2 * width * message,
    )(normed, *weights)


def own_index(axis):
    return lax.axis_index(axis).astype(jnp.int32).reshape(1)


def fetch(block, per_block, slots, side, here, other, target, sem):
    stored_here = here.shape[0]
    slot = slots[per_block[block]]
    at = lax.rem(slot, jnp.int32(stored_here))
    mine = lax.div(slot, jnp.int32(stored_here)) == side[0]

    @pl.when(mine)
    def _():
        pltpu.make_async_copy(here.at[at], target.at[block], sem.at[block]).start()

    @pl.when(jnp.logical_not(mine))
    def _():
        pltpu.make_async_copy(other.at[at], target.at[block], sem.at[block]).start()

    return pltpu.make_async_copy(here.at[0], target.at[block], sem.at[block])


def add_adapters(message, adapters, stores, others, blocks):
    shares, own, width = message.shape
    _, rank, columns = stores[0].shape
    lead = rank // own * columns

    def body(per_block, slots, side, m, down, up, other_down, other_up, out, ups, piece, sem):
        waits = [
            fetch(b, per_block, slots, side, here, other, target, sem.at[n])
            for b in range(blocks)
            for n, (here, other, target) in enumerate(
                ((down, other_down, piece), (up, other_up, ups))
            )
        ]
        for j in range(shares):
            out[j, :, lead:] = m[j]
        for wait in waits:
            wait.wait()
        for b in range(blocks):
            lines = [
                piece[b, m * own : (m + 1) * own, :].astype(f32) for m in range(rank // own)
            ]
            packed = jnp.concatenate(lines, axis=1).astype(bf16)
            for j in range(b * BLOCK // own, (b + 1) * BLOCK // own):
                out[j, :, :lead] = packed

    smem = whole(pltpu.SMEM)
    return pl.pallas_call(
        body,
        out_shape=(
            jax.ShapeDtypeStruct((shares, own, lead + width), bf16),
            jax.ShapeDtypeStruct((blocks,) + stores[1].shape[1:], bf16),
        ),
        in_specs=[smem, smem, smem, whole()] + [whole(pltpu.HBM)] * 4,
        out_specs=(whole(), whole()),
        scratch_shapes=[
            pltpu.VMEM((blocks, rank, columns), bf16),
            pltpu.SemaphoreType.DMA((2, blocks)),
        ],
        compiler_params=pltpu.CompilerParams(vmem_limit_bytes=16 * MIB),
    )(*adapters, message, *map(far, stores), *map(far, others))


def attend(arrived, pairs, older, lengths, cache, down, step, lead, rank):
    shares, own, message = arrived.shape
    context, width = cache.shape[1:]
    half = width // 2
    query_width = QUERY_HEAD_COUNT * HEAD_SIZE // shares
    per_share = query_width // HEAD_SIZE
    groups = QUERY_HEAD_COUNT // KV_HEADS
    pair_inside = pairs is None

    def body(*refs):
        refs = list(refs)
        lens, x = refs.pop(0), refs.pop(0)
        pair_ref = None if pair_inside else refs.pop(0)
        old = refs.pop(0) if step else None
        kv = refs.pop(0)
        if step:
            down_ref, out, new = refs
        else:
            out, new, down_ref = refs
            for j in range(shares):
                lines = [
                    x[j, :, m * query_width : (m + 1) * query_width].astype(f32)
                    for m in range(rank // own)
                ]
                down_ref[j] = jnp.concatenate(lines, axis=0).astype(bf16)
        half_head = HEAD_SIZE // 2
        lane = lax.broadcasted_iota(jnp.int32, (1, HEAD_SIZE), 1)
        entry = jnp.where(lane < half_head, lane, lane - half_head).astype(f32)
        frequency = jnp.exp(entry * f32(-2.0 / HEAD_SIZE * math.log(rope_base)))
        place = lax.broadcasted_iota(jnp.int32, (groups, context), 1)
        rows = [x[j, :, lead:].astype(f32) for j in range(shares)]
        outputs = []
        fresh = []
        for r in range(own):
            angle = (lens[r] + step).astype(f32) * frequency
            cosine = jnp.cos(angle)
            sine = jnp.where(lane < half_head, -jnp.sin(angle), jnp.sin(angle))

            def turn(v):
                return v * cosine + pltpu.roll(v, HEAD_SIZE // 2, 1) * sine

            def pair_head(c):
                if pair_inside:
                    return rows[c][r : r + 1, query_width:]
                return pair_ref[r : r + 1, c * HEAD_SIZE : (c + 1) * HEAD_SIZE].astype(f32)

            heads = []
            line = []
            for g in range(KV_HEADS):
                line.append(turn(pair_head(g)).astype(bf16))
            for g in range(KV_HEADS):
                line.append(pair_head(KV_HEADS + g).astype(bf16))
            fresh.append(jnp.concatenate([v.astype(f32) for v in line], axis=1))
            for g in range(KV_HEADS):
                column = slice(g * HEAD_SIZE, (g + 1) * HEAD_SIZE)
                value_column = slice(half + g * HEAD_SIZE, half + (g + 1) * HEAD_SIZE)
                lines = []
                for h in range(g * groups, (g + 1) * groups):
                    at = (h % per_share) * HEAD_SIZE
                    lines.append(rows[h // per_share][r : r + 1, at : at + HEAD_SIZE])
                query = turn(jnp.concatenate(lines, axis=0)).astype(bf16)
                scores = lax.dot_general(
                    query, kv[r, :, column], (((1,), (1,)), ((), ())), preferred_element_type=f32
                ) * (1.0 / math.sqrt(HEAD_SIZE))
                scores = jnp.where(place < lens[r], scores, f32(-1e30))
                new_keys = [line[g].astype(f32)]
                new_values = [line[KV_HEADS + g].astype(f32)]
                if step:
                    new_keys.append(old[r : r + 1, column].astype(f32))
                    new_values.append(old[r : r + 1, value_column].astype(f32))
                wide_query = query.astype(f32)
                extra = [
                    jnp.sum(wide_query * k, axis=1, keepdims=True) * (1.0 / math.sqrt(HEAD_SIZE))
                    for k in new_keys
                ]
                peak = jnp.max(scores, axis=1, keepdims=True)
                for e in extra:
                    peak = jnp.maximum(peak, e)
                weight = jnp.exp(scores - peak)
                extra = [jnp.exp(e - peak) for e in extra]
                total = jnp.sum(weight, axis=1, keepdims=True)
                for e in extra:
                    total = total + e
                result = jnp.dot(
                    (weight / total).astype(bf16), kv[r, :, value_column], preferred_element_type=f32
                )
                for e, v in zip(extra, new_values):
                    result = result + (e / total).astype(bf16).astype(f32) * v
                heads.append(result)
            outputs.append(heads)
        fresh = jnp.concatenate(fresh, axis=0).astype(bf16)
        if step < STEPS - 1:
            new[...] = fresh
        else:
            new[0] = old[...]
            new[1] = fresh
        low = jnp.zeros((own, rank), f32)
        for j in range(shares):
            lines = []
            for r in range(own):
                cells = []
                for h in range(j * per_share, (j + 1) * per_share):
                    at = h % groups
                    cells.append(outputs[r][h // groups][at : at + 1, :])
                lines.append(jnp.concatenate(cells, axis=1))
            share = jnp.concatenate(lines, axis=0).astype(bf16)
            out[j, :, :query_width] = share
            low = low + lax.dot_general(
                share, down_ref[j], (((1,), (1,)), ((), ())), preferred_element_type=f32
            )
        padded = jnp.concatenate([low, jnp.zeros((own, HEAD_SIZE - rank), f32)], axis=1).astype(bf16)
        for j in range(shares):
            out[j, :, query_width:] = padded

    operands = [lengths, arrived]
    specs = [whole(pltpu.SMEM), whole()]
    for extra in ([] if pair_inside else [pairs]) + ([older] if step else []):
        operands.append(extra)
        specs.append(whole())
    operands += [cache] + ([down] if step else [])
    specs += [whole()] * (2 if step else 1)
    outs = [
        jax.ShapeDtypeStruct((shares, own, query_width + HEAD_SIZE), bf16),
        jax.ShapeDtypeStruct((own, width) if step < STEPS - 1 else (STEPS, own, width), bf16),
    ]
    if not step:
        outs.append(jax.ShapeDtypeStruct((shares, rank, query_width), bf16))
    return pl.pallas_call(
        body,
        out_shape=tuple(outs),
        in_specs=specs,
        out_specs=(whole(),) * len(outs),
        compiler_params=pltpu.CompilerParams(vmem_limit_bytes=16 * MIB),
        cost_estimate=pl.CostEstimate(
            flops=8 * own * QUERY_HEAD_COUNT * HEAD_SIZE * context,
            bytes_accessed=2 * own * context * width,
            transcendentals=0,
        ),
    )(*operands)


def output_terms(arrived, output_weight, up):
    shares, own, _ = arrived.shape
    query_width, width = output_weight.shape
    blocks, rank, share_width = up.shape
    rows = shares * own
    step = 1024

    def body(mine, x, wo, up_ref, out, added):
        heads = rows_of(x, 0, query_width)
        low = rows_of(x, query_width, HEAD_SIZE)[:, :rank]
        added[...] = jnp.zeros_like(added)
        start = pl.multiple_of(mine[0] * share_width, share_width)
        for b in range(blocks):
            lines = slice(b * BLOCK, (b + 1) * BLOCK)
            added[lines, pl.ds(start, share_width)] = jnp.dot(
                low[lines], up_ref[b], preferred_element_type=f32
            )
        for i in range(width // step):
            columns = slice(i * step, (i + 1) * step)
            total = added[:, columns] + jnp.dot(
                heads, wo[:, columns], preferred_element_type=f32
            )
            for j in range(shares):
                out[j, :, columns] = total[j * own : (j + 1) * own, :].astype(out.dtype)

    return pl.pallas_call(
        body,
        out_shape=jax.ShapeDtypeStruct((shares, own, width), term_type),
        in_specs=[whole(pltpu.SMEM)] + [whole()] * 3,
        out_specs=whole(),
        scratch_shapes=[pltpu.VMEM((rows, width), f32)],
        compiler_params=pltpu.CompilerParams(vmem_limit_bytes=16 * MIB),
        cost_estimate=cost(2 * rows * width * query_width, 2 * width * query_width),
    )(own_index("tp"), arrived, output_weight, up)


def close_step(terms, hidden, scale):
    shares, own, width = terms.shape
    normed = scale is not None

    def body(t, h, *refs):
        total = h[...].astype(f32)
        for j in range(shares):
            total = total + t[j].astype(f32)
        rounded = total.astype(bf16)
        spread = rounded
        if normed:
            s, out, kept = refs
            kept[...] = rounded
            wide = rounded.astype(f32)
            mean = jnp.mean(wide * wide, axis=-1, keepdims=True)
            wide = wide * lax.rsqrt(mean + norm_epsilon)
            gain = s[...].astype(f32)
            spread = jnp.concatenate(
                [
                    wide[:, c * HEAD_SIZE : (c + 1) * HEAD_SIZE] * gain[c : c + 1, :]
                    for c in range(width // HEAD_SIZE)
                ],
                axis=1,
            ).astype(bf16)
        else:
            (out,) = refs
        for j in range(shares):
            out[j] = spread

    outs = [jax.ShapeDtypeStruct((shares, own, width), bf16)]
    operands = [terms, hidden]
    if normed:
        outs.append(jax.ShapeDtypeStruct((own, width), bf16))
        operands.append(scale)
    return call(
        body, tuple(outs), [whole()] * len(operands), 8 * own * width, 6 * shares * own * width
    )(*operands)


def exchange(chunks):
    return lax.all_to_all(chunks, "tp", split_axis=0, concat_axis=0, tiled=True)


def local(
    input_hidden_rows,
    input_norm_scale,
    query_weight,
    key_value_weight,
    output_weight,
    cache,
    lengths,
    adapter_per_block,
    adapter_storage_slot,
    adapter_down_projection,
    adapter_up_projection,
):
    rows_req = input_hidden_rows.shape[0]
    own = cache.shape[0]
    blocks = rows_req // BLOCK
    width = input_hidden_rows.shape[1]
    query_width = query_weight.shape[1]
    rank = adapter_down_projection.shape[1]
    scale = input_norm_scale.reshape(width // HEAD_SIZE, HEAD_SIZE)
    adapters = (
        adapter_per_block,
        adapter_storage_slot,
        own_index("req"),
    )
    cores = [(0, 1), (1, 0)]
    stores = (adapter_down_projection, adapter_up_projection)
    others = [lax.ppermute(store, "req", cores) for store in stores]
    lead = rank // own * query_width
    weights = (query_weight, key_value_weight)
    message, hidden = first_projection(input_hidden_rows, scale, weights, own)
    message, up = add_adapters(message, adapters, stores, others, blocks)
    down = fresh = None
    for step in range(STEPS):
        arrived = exchange(message)
        start = 0 if step else lead
        pairs = None
        if key_value_weight.shape[1] != HEAD_SIZE:
            pairs = arrived[:, :, start + query_width :].transpose(1, 0, 2).reshape(own, -1)
        attended, fresh, *first = attend(
            arrived, pairs, fresh, lengths, cache, down, step, start, rank
        )
        if not step:
            (down,) = first
        terms = exchange(output_terms(exchange(attended), output_weight, up))
        if step < STEPS - 1:
            spread, hidden = close_step(terms, hidden, scale)
            message = next_projection(exchange(spread), weights)
        else:
            (spread,) = close_step(terms, hidden, None)
    return (exchange(spread).reshape(rows_req, width), fresh)


def solution(mesh):
    in_specs = (
        P(("parts", "req"), None),
        P(),
        P(None, "tp"),
        P(None, "tp"),
        P("tp", None),
        P(("parts", "req", "tp"), None, None),
        P(("parts", "req", "tp")),
        P(("parts", "req")),
        P(),
        P("req", None, "tp"),
        P("req", None, "tp"),
    )
    out_specs = (P(("parts", "req"), None), P(None, ("parts", "req", "tp"), None))
    return jax.shard_map(local, mesh=mesh, in_specs=in_specs, out_specs=out_specs, check_vma=False)
```

```python
import math

import jax
import jax.numpy as jnp
from jax import lax
from jax.experimental import pallas as pl
from jax.experimental.pallas import tpu as pltpu
from jax.sharding import PartitionSpec as P

MODEL_WIDTH = 8192
HEAD_SIZE = 128
QUERY_HEAD_COUNT = 32
KV_HEADS = 4
BLOCK = 16
STEPS = 2

rope_base = 500000.0
norm_epsilon = 1e-05
term_type = jnp.bfloat16
f32 = jnp.float32
bf16 = jnp.bfloat16
MIB = 1 << 20
FIRST = 24


def whole(kind=pltpu.VMEM):
    return pl.BlockSpec(memory_space=kind)


def call(body, outs, ins, flops, data_bytes, limit=16):
    return pl.pallas_call(
        body,
        out_shape=outs,
        in_specs=ins,
        out_specs=jax.tree.map(lambda _: whole(), outs),
        compiler_params=pltpu.CompilerParams(vmem_limit_bytes=limit * MIB),
        cost_estimate=pl.CostEstimate(flops=flops, bytes_accessed=data_bytes, transcendentals=0),
    )


def far(array):
    return pltpu.with_memory_space_constraint(array, pltpu.HBM)


def rows_of(ref, start, width):
    pieces = [ref[j, :, pl.ds(start, width)].astype(f32) for j in range(ref.shape[0])]
    return jnp.concatenate(pieces, axis=0).astype(bf16)


def pieces_of(depth):
    unit = depth // 8
    bounds = [0, 3 * unit, 6 * unit, 7 * unit, depth]
    return list(zip(bounds[:-1], bounds[1:]))


def project(weights, chunk_of, rows, pieces, ready=None):
    sums = [jnp.zeros((rows, w.shape[1]), f32) for w in weights]
    for i, (start, stop) in enumerate(pieces):
        if ready is not None:
            ready(i)
        part = chunk_of(start, stop - start)
        sums = [
            total + jnp.dot(part, w[start:stop, :], preferred_element_type=f32)
            for total, w in zip(sums, weights)
        ]
    return sums


def store_shares(out, query, pair):
    shares, own, _ = out.shape
    width = query.shape[1]
    for j in range(shares):
        lines = slice(j * own, (j + 1) * own)
        out[j, :, :width] = query[lines].astype(bf16)
        out[j, :, width:] = pair[lines].astype(bf16)


def cost(flops, data_bytes):
    return pl.CostEstimate(flops=flops, bytes_accessed=data_bytes, transcendentals=0)


def first_projection(source, scale, weights, own):
    rows, width = source.shape
    shares = rows // own
    message = sum(w.shape[1] for w in weights)
    pieces = pieces_of(width)

    def body(mine, source_ref, s, wq, wp, out, held, *scratch):
        kept_q, kept_p, sems, x, gains, wide, normed, pre = scratch
        loads = [
            pltpu.make_async_copy(source_ref, x, pre.at[0]),
            pltpu.make_async_copy(s, gains, pre.at[1]),
        ]
        for load in loads:
            load.start()
        copies = [
            [
                pltpu.make_async_copy(w.at[start:stop, :], k.at[start:stop, :], sems.at[n, i])
                for n, (w, k) in enumerate(((wq, kept_q), (wp, kept_p)))
            ]
            for i, (start, stop) in enumerate(pieces)
        ]
        for pair in copies:
            for copy in pair:
                copy.start()

        def ready(i):
            for copy in copies[i]:
                copy.wait()

        for load in loads:
            load.wait()
        wide[...] = x[...].astype(f32)
        lines = wide[:own, :]
        for j in range(1, shares):
            lines = jnp.where(mine[0] == j, wide[j * own : (j + 1) * own, :], lines)
        held[...] = lines.astype(bf16)
        value = wide[...]
        ratio = lax.rsqrt(jnp.mean(value * value, axis=-1, keepdims=True) + norm_epsilon)
        gain = gains[...].astype(f32)
        for c in range(width // HEAD_SIZE):
            columns = slice(c * HEAD_SIZE, (c + 1) * HEAD_SIZE)
            normed[:, columns] = (wide[:, columns] * ratio * gain[c : c + 1, :]).astype(bf16)
        sums = project(
            (kept_q, kept_p), lambda at, n: normed[:, at : at + n], rows, pieces, ready
        )
        store_shares(out, *sums)

    return pl.pallas_call(
        body,
        out_shape=(
            jax.ShapeDtypeStruct((shares, own, message), bf16),
            jax.ShapeDtypeStruct((own, width), bf16),
        ),
        in_specs=[whole(pltpu.SMEM)] + [whole(pltpu.HBM)] * 4,
        out_specs=(whole(), whole()),
        scratch_shapes=[pltpu.VMEM(w.shape, bf16) for w in weights]
        + [
            pltpu.SemaphoreType.DMA((2, len(pieces))),
            pltpu.VMEM(source.shape, bf16),
            pltpu.VMEM(scale.shape, bf16),
            pltpu.VMEM(source.shape, f32),
            pltpu.VMEM(source.shape, bf16),
            pltpu.SemaphoreType.DMA((2,)),
        ],
        compiler_params=pltpu.CompilerParams(vmem_limit_bytes=FIRST * MIB),
        cost_estimate=cost(2 * rows * width * message, 2 * width * message),
    )(own_index("tp"), far(source), far(scale), *map(far, weights))


def next_projection(normed, weights):
    shares, own, width = normed.shape
    message = sum(w.shape[1] for w in weights)

    def body(x, wq, wp, out):
        pieces = [(at, at + 1024) for at in range(0, width, 1024)]
        store_shares(out, *project((wq, wp), lambda at, n: rows_of(x, at, n), shares * own, pieces))

    return call(
        body,
        jax.ShapeDtypeStruct((shares, own, message), bf16),
        [whole()] * 3,
        2 * shares * own * width * message,
        2 * width * message,
    )(normed, *weights)


def own_index(axis):
    return lax.axis_index(axis).astype(jnp.int32).reshape(1)


def fetch(block, per_block, slots, side, here, other, target, sem):
    stored_here = here.shape[0]
    slot = slots[per_block[block]]
    at = lax.rem(slot, jnp.int32(stored_here))
    mine = lax.div(slot, jnp.int32(stored_here)) == side[0]

    @pl.when(mine)
    def _():
        pltpu.make_async_copy(here.at[at], target.at[block], sem.at[block]).start()

    @pl.when(jnp.logical_not(mine))
    def _():
        pltpu.make_async_copy(other.at[at], target.at[block], sem.at[block]).start()

    return pltpu.make_async_copy(here.at[0], target.at[block], sem.at[block])


def add_down(message, adapters, here, other, lengths, blocks):
    shares, own, width = message.shape
    _, rank, columns = here.shape
    lead = rank // own * columns

    def body(per_block, slots, side, lens, m, here_ref, other_ref, out, turns, piece, sem):
        waits = [
            fetch(b, per_block, slots, side, here_ref, other_ref, piece, sem)
            for b in range(blocks)
        ]
        for j in range(shares):
            out[j, :, lead:] = m[j]
        half_head = HEAD_SIZE // 2
        lane = lax.broadcasted_iota(jnp.int32, (STEPS * own, HEAD_SIZE), 1)
        line = lax.broadcasted_iota(jnp.int32, (STEPS * own, HEAD_SIZE), 0)
        position = jnp.zeros_like(line)
        for n in range(STEPS * own):
            position = jnp.where(line == n, lens[n % own] + n // own, position)
        entry = jnp.where(lane < half_head, lane, lane - half_head).astype(f32)
        angle = position.astype(f32) * jnp.exp(entry * f32(-2.0 / HEAD_SIZE * math.log(rope_base)))
        sine = jnp.sin(angle)
        turns[0] = jnp.cos(angle)
        turns[1] = jnp.where(lane < half_head, -sine, sine)
        for wait in waits:
            wait.wait()
        for b in range(blocks):
            lines = [
                piece[b, m * own : (m + 1) * own, :].astype(f32) for m in range(rank // own)
            ]
            packed = jnp.concatenate(lines, axis=1).astype(bf16)
            for j in range(b * BLOCK // own, (b + 1) * BLOCK // own):
                out[j, :, :lead] = packed

    smem = whole(pltpu.SMEM)
    return pl.pallas_call(
        body,
        out_shape=(
            jax.ShapeDtypeStruct((shares, own, lead + width), bf16),
            jax.ShapeDtypeStruct((2, STEPS * own, HEAD_SIZE), f32),
        ),
        in_specs=[smem] * 4 + [whole(), whole(pltpu.HBM), whole(pl.ANY)],
        out_specs=(whole(), whole()),
        scratch_shapes=[
            pltpu.VMEM((blocks, rank, columns), bf16),
            pltpu.SemaphoreType.DMA((blocks,)),
        ],
        compiler_params=pltpu.CompilerParams(vmem_limit_bytes=16 * MIB),
    )(*adapters, lengths, message, far(here), other)


def attend(arrived, pairs, older, turns, lengths, cache, adapters, stores, step, lead, rank):
    shares, own, message = arrived.shape
    context, width = cache.shape[1:]
    half = width // 2
    query_width = QUERY_HEAD_COUNT * HEAD_SIZE // shares
    per_share = query_width // HEAD_SIZE
    groups = QUERY_HEAD_COUNT // KV_HEADS
    lines = groups * own
    pair_inside = pairs is None
    first, last = step == 0, step == STEPS - 1
    shrink = 1.0 / math.sqrt(HEAD_SIZE)

    def body(*refs):
        refs = list(refs)
        lens, x = refs.pop(0), refs.pop(0)
        pair_ref = None if pair_inside else refs.pop(0)
        old = None if first else refs.pop(0)
        turn_ref, kv = refs.pop(0), refs.pop(0)
        if first:
            per_block, slots, side, here, other, out, new, down_ref, ups, sem = refs
            waits = [
                fetch(b, per_block, slots, side, here, other, ups, sem)
                for b in range(ups.shape[0])
            ]
            for j in range(shares):
                pieces = [
                    x[j, :, m * query_width : (m + 1) * query_width].astype(f32)
                    for m in range(rank // own)
                ]
                down_ref[j] = jnp.concatenate(pieces, axis=0).astype(bf16)
        else:
            down_ref, out, new = refs
        cosine = turn_ref[0, step * own : (step + 1) * own, :]
        sine = turn_ref[1, step * own : (step + 1) * own, :]
        row_of = lax.rem(lax.broadcasted_iota(jnp.int32, (lines, 1), 0), own)

        def by_row(values):
            result = values[0]
            for r in range(1, own):
                result = jnp.where(row_of == r, values[r], result)
            return result

        def spread(rows):
            return by_row([rows[r : r + 1, :] for r in range(own)])

        def turn(v, c, s):
            return v * c + pltpu.roll(v, HEAD_SIZE // 2, 1) * s

        def pair_head(c):
            if pair_inside:
                return x[c, :, lead + query_width :].astype(f32)
            return pair_ref[:, c * HEAD_SIZE : (c + 1) * HEAD_SIZE].astype(f32)

        keys = [turn(pair_head(g), cosine, sine).astype(bf16) for g in range(KV_HEADS)]
        values = [pair_head(KV_HEADS + g).astype(bf16) for g in range(KV_HEADS)]
        fresh = jnp.concatenate(keys + values, axis=1)
        if last:
            new[0] = old[...]
            new[1] = fresh
        else:
            new[...] = fresh
        wide_cosine, wide_sine = spread(cosine), spread(sine)
        valid = lax.broadcasted_iota(jnp.int32, (lines, context), 1) < by_row(
            [jnp.full((lines, 1), lens[r], jnp.int32) for r in range(own)]
        )
        scores = []
        extras = []
        new_values = []
        for g in range(KV_HEADS):
            column = slice(g * HEAD_SIZE, (g + 1) * HEAD_SIZE)
            value_column = slice(half + g * HEAD_SIZE, half + (g + 1) * HEAD_SIZE)
            pieces = []
            for h in range(g * groups, (g + 1) * groups):
                at = lead + (h % per_share) * HEAD_SIZE
                pieces.append(x[h // per_share, :, at : at + HEAD_SIZE].astype(f32))
            query = turn(jnp.concatenate(pieces, axis=0), wide_cosine, wide_sine).astype(bf16)
            score = by_row(
                [
                    lax.dot_general(
                        query, kv[r, :, column], (((1,), (1,)), ((), ())), preferred_element_type=f32
                    )
                    for r in range(own)
                ]
            )
            scores.append(jnp.where(valid, score * shrink, f32(-1e30)))
            added = [(keys[g], values[g])]
            if not first:
                added.append((old[:, column], old[:, value_column]))
            wide_query = query.astype(f32)
            extras.append(
                [
                    jnp.sum(wide_query * spread(k.astype(f32)), axis=1, keepdims=True) * shrink
                    for k, _ in added
                ]
            )
            new_values.append([spread(v.astype(f32)) for _, v in added])
        results = []
        for g in range(KV_HEADS):
            value_column = slice(half + g * HEAD_SIZE, half + (g + 1) * HEAD_SIZE)
            peak = jnp.max(scores[g], axis=1, keepdims=True)
            for e in extras[g]:
                peak = jnp.maximum(peak, e)
            weight = jnp.exp(scores[g] - peak)
            more = [jnp.exp(e - peak) for e in extras[g]]
            total = jnp.sum(weight, axis=1, keepdims=True)
            for e in more:
                total = total + e
            probs = (weight / total).astype(bf16)
            result = by_row(
                [
                    jnp.dot(probs, kv[r, :, value_column], preferred_element_type=f32)
                    for r in range(own)
                ]
            )
            for e, v in zip(more, new_values[g]):
                result = result + (e / total).astype(bf16).astype(f32) * v
            results.append(result)
        low = jnp.zeros((own, rank), f32)
        for j in range(shares):
            cells = []
            for h in range(j * per_share, (j + 1) * per_share):
                at = h % groups * own
                cells.append(results[h // groups][at : at + own, :])
            share = jnp.concatenate(cells, axis=1).astype(bf16)
            out[j, :, :query_width] = share
            low = low + lax.dot_general(
                share, down_ref[j], (((1,), (1,)), ((), ())), preferred_element_type=f32
            )
        padded = jnp.concatenate([low, jnp.zeros((own, HEAD_SIZE - rank), f32)], axis=1).astype(bf16)
        for j in range(shares):
            out[j, :, query_width:] = padded
        if first:
            for wait in waits:
                wait.wait()

    smem = whole(pltpu.SMEM)
    operands = [lengths, arrived]
    specs = [smem, whole()]
    for extra in ([] if pair_inside else [pairs]) + ([] if first else [older]) + [turns, cache]:
        operands.append(extra)
        specs.append(whole())
    outs = [
        jax.ShapeDtypeStruct((shares, own, query_width + HEAD_SIZE), bf16),
        jax.ShapeDtypeStruct((STEPS, own, width) if last else (own, width), bf16),
    ]
    scratch = []
    if first:
        operands += [*adapters, far(stores[0]), stores[1]]
        specs += [smem] * 3 + [whole(pltpu.HBM), whole(pl.ANY)]
        blocks = adapters[0].shape[0]
        outs.append(jax.ShapeDtypeStruct((shares, rank, query_width), bf16))
        outs.append(jax.ShapeDtypeStruct((blocks,) + stores[0].shape[1:], bf16))
        scratch.append(pltpu.SemaphoreType.DMA((blocks,)))
    else:
        operands.append(stores)
        specs.append(whole())
    return pl.pallas_call(
        body,
        out_shape=tuple(outs),
        in_specs=specs,
        out_specs=(whole(),) * len(outs),
        scratch_shapes=scratch,
        compiler_params=pltpu.CompilerParams(vmem_limit_bytes=16 * MIB),
        cost_estimate=cost(
            8 * own * QUERY_HEAD_COUNT * HEAD_SIZE * context, 2 * own * context * width
        ),
    )(*operands)


def output_terms(arrived, output_weight, up):
    shares, own, _ = arrived.shape
    query_width, width = output_weight.shape
    blocks, rank, share_width = up.shape
    rows = shares * own
    step = 1024

    def body(mine, x, wo, up_ref, out, added):
        heads = rows_of(x, 0, query_width)
        low = rows_of(x, query_width, HEAD_SIZE)[:, :rank]
        added[...] = jnp.zeros_like(added)
        start = pl.multiple_of(mine[0] * share_width, share_width)
        for b in range(blocks):
            lines = slice(b * BLOCK, (b + 1) * BLOCK)
            added[lines, pl.ds(start, share_width)] = jnp.dot(
                low[lines], up_ref[b], preferred_element_type=f32
            )
        for i in range(width // step):
            columns = slice(i * step, (i + 1) * step)
            total = added[:, columns] + jnp.dot(
                heads, wo[:, columns], preferred_element_type=f32
            )
            for j in range(shares):
                out[j, :, columns] = total[j * own : (j + 1) * own, :].astype(out.dtype)

    return pl.pallas_call(
        body,
        out_shape=jax.ShapeDtypeStruct((shares, own, width), term_type),
        in_specs=[whole(pltpu.SMEM)] + [whole()] * 3,
        out_specs=whole(),
        scratch_shapes=[pltpu.VMEM((rows, width), f32)],
        compiler_params=pltpu.CompilerParams(vmem_limit_bytes=16 * MIB),
        cost_estimate=cost(2 * rows * width * query_width, 2 * width * query_width),
    )(own_index("tp"), arrived, output_weight, up)


def close_step(terms, hidden, scale):
    shares, own, width = terms.shape
    normed = scale is not None

    def body(t, h, *refs):
        total = h[...].astype(f32)
        for j in range(shares):
            total = total + t[j].astype(f32)
        rounded = total.astype(bf16)
        spread = rounded
        if normed:
            s, out, kept = refs
            kept[...] = rounded
            wide = rounded.astype(f32)
            mean = jnp.mean(wide * wide, axis=-1, keepdims=True)
            wide = wide * lax.rsqrt(mean + norm_epsilon)
            gain = s[...].astype(f32)
            spread = jnp.concatenate(
                [
                    wide[:, c * HEAD_SIZE : (c + 1) * HEAD_SIZE] * gain[c : c + 1, :]
                    for c in range(width // HEAD_SIZE)
                ],
                axis=1,
            ).astype(bf16)
        else:
            (out,) = refs
        for j in range(shares):
            out[j] = spread

    outs = [jax.ShapeDtypeStruct((shares, own, width), bf16)]
    operands = [terms, hidden]
    if normed:
        outs.append(jax.ShapeDtypeStruct((own, width), bf16))
        operands.append(scale)
    return call(
        body, tuple(outs), [whole()] * len(operands), 8 * own * width, 6 * shares * own * width
    )(*operands)


def exchange(chunks):
    return lax.all_to_all(chunks, "tp", split_axis=0, concat_axis=0, tiled=True)


def local(
    input_hidden_rows,
    input_norm_scale,
    query_weight,
    key_value_weight,
    output_weight,
    cache,
    lengths,
    adapter_per_block,
    adapter_storage_slot,
    adapter_down_projection,
    adapter_up_projection,
):
    rows_req = input_hidden_rows.shape[0]
    own = cache.shape[0]
    blocks = rows_req // BLOCK
    width = input_hidden_rows.shape[1]
    query_width = query_weight.shape[1]
    rank = adapter_down_projection.shape[1]
    scale = input_norm_scale.reshape(width // HEAD_SIZE, HEAD_SIZE)
    adapters = (
        adapter_per_block,
        adapter_storage_slot,
        own_index("req"),
    )
    cores = [(0, 1), (1, 0)]
    other_down = lax.ppermute(adapter_down_projection, "req", cores)
    other_up = lax.ppermute(adapter_up_projection, "req", cores)
    lead = rank // own * query_width
    weights = (query_weight, key_value_weight)
    message, hidden = first_projection(input_hidden_rows, scale, weights, own)
    message, turns = add_down(
        message, adapters, adapter_down_projection, other_down, lengths, blocks
    )
    down = fresh = None
    for step in range(STEPS):
        arrived = exchange(message)
        start = 0 if step else lead
        pairs = None
        if key_value_weight.shape[1] != HEAD_SIZE:
            pairs = arrived[:, :, start + query_width :].transpose(1, 0, 2).reshape(own, -1)
        stores = down if step else (adapter_up_projection, other_up)
        attended, fresh, *kept = attend(
            arrived, pairs, fresh, turns, lengths, cache, adapters, stores, step, start, rank
        )
        if not step:
            down, up = kept
        terms = exchange(output_terms(exchange(attended), output_weight, up))
        if step < STEPS - 1:
            spread, hidden = close_step(terms, hidden, scale)
            message = next_projection(exchange(spread), weights)
        else:
            (spread,) = close_step(terms, hidden, None)
    return (exchange(spread).reshape(rows_req, width), fresh)


def solution(mesh):
    in_specs = (
        P(("parts", "req"), None),
        P(),
        P(None, "tp"),
        P(None, "tp"),
        P("tp", None),
        P(("parts", "req", "tp"), None, None),
        P(("parts", "req", "tp")),
        P(("parts", "req")),
        P(),
        P("req", None, "tp"),
        P("req", None, "tp"),
    )
    out_specs = (P(("parts", "req"), None), P(None, ("parts", "req", "tp"), None))
    return jax.shard_map(local, mesh=mesh, in_specs=in_specs, out_specs=out_specs, check_vma=False)
```

```python
import math

import jax
import jax.numpy as jnp
from jax import lax
from jax.experimental import pallas as pl
from jax.experimental.pallas import tpu as pltpu
from jax.sharding import PartitionSpec as P

MODEL_WIDTH = 8192
HEAD_SIZE = 128
QUERY_HEAD_COUNT = 32
KV_HEADS = 4
BLOCK = 16
STEPS = 2

rope_base = 500000.0
norm_epsilon = 1e-05
term_type = jnp.bfloat16
f32 = jnp.float32
bf16 = jnp.bfloat16
MIB = 1 << 20


def whole(kind=pltpu.VMEM):
    return pl.BlockSpec(memory_space=kind)


def call(body, outs, ins, flops, data_bytes, limit=16):
    return pl.pallas_call(
        body,
        out_shape=outs,
        in_specs=ins,
        out_specs=jax.tree.map(lambda _: whole(), outs),
        compiler_params=pltpu.CompilerParams(vmem_limit_bytes=limit * MIB),
        cost_estimate=pl.CostEstimate(flops=flops, bytes_accessed=data_bytes, transcendentals=0),
    )


def far(array):
    return pltpu.with_memory_space_constraint(array, pltpu.HBM)


def rows_of(ref, start, width):
    pieces = [ref[j, :, pl.ds(start, width)].astype(f32) for j in range(ref.shape[0])]
    return jnp.concatenate(pieces, axis=0).astype(bf16)


def pieces_of(depth, count):
    return [(i * depth // count, (i + 1) * depth // count) for i in range(count)]


def project(weights, chunk_of, rows, pieces, ready=None):
    sums = [jnp.zeros((rows, w.shape[1]), f32) for w in weights]
    for i, (start, stop) in enumerate(pieces):
        if ready is not None:
            ready(i)
        part = chunk_of(start, stop - start)
        sums = [
            total + jnp.dot(part, w[start:stop, :], preferred_element_type=f32)
            for total, w in zip(sums, weights)
        ]
    return sums


def store_shares(out, query, pair):
    shares, own, _ = out.shape
    width = query.shape[1]
    for j in range(shares):
        lines = slice(j * own, (j + 1) * own)
        out[j, :, :width] = query[lines].astype(bf16)
        out[j, :, width:] = pair[lines].astype(bf16)


def cost(flops, data_bytes):
    return pl.CostEstimate(flops=flops, bytes_accessed=data_bytes, transcendentals=0)


def first_projection(source, scale, weights, own):
    rows, width = source.shape
    shares = rows // own
    message = sum(w.shape[1] for w in weights)
    pieces = pieces_of(width, 4)
    ahead = 2

    def body(mine, source_ref, s, wq, wp, out, held, *scratch):
        kept_q, kept_p, sems, x, gains, wide, normed, pre = scratch
        loads = [
            pltpu.make_async_copy(source_ref, x, pre.at[0]),
            pltpu.make_async_copy(s, gains, pre.at[1]),
        ]
        for load in loads:
            load.start()
        copies = [
            [
                pltpu.make_async_copy(w.at[start:stop, :], k.at[start:stop, :], sems.at[n, i])
                for n, (w, k) in enumerate(((wq, kept_q), (wp, kept_p)))
            ]
            for i, (start, stop) in enumerate(pieces)
        ]
        for pair in copies[:ahead]:
            for copy in pair:
                copy.start()

        def ready(i):
            for copy in copies[i]:
                copy.wait()
            for copy in copies[i + ahead] if i + ahead < len(copies) else []:
                copy.start()

        for load in loads:
            load.wait()
        wide[...] = x[...].astype(f32)
        lines = wide[:own, :]
        for j in range(1, shares):
            lines = jnp.where(mine[0] == j, wide[j * own : (j + 1) * own, :], lines)
        held[...] = lines.astype(bf16)
        value = wide[...]
        ratio = lax.rsqrt(jnp.mean(value * value, axis=-1, keepdims=True) + norm_epsilon)
        gain = gains[...].astype(f32)
        for c in range(width // HEAD_SIZE):
            columns = slice(c * HEAD_SIZE, (c + 1) * HEAD_SIZE)
            normed[:, columns] = (wide[:, columns] * ratio * gain[c : c + 1, :]).astype(bf16)
        sums = project(
            (kept_q, kept_p), lambda at, n: normed[:, at : at + n], rows, pieces, ready
        )
        store_shares(out, *sums)

    return pl.pallas_call(
        body,
        out_shape=(
            jax.ShapeDtypeStruct((shares, own, message), bf16),
            jax.ShapeDtypeStruct((own, width), bf16),
        ),
        in_specs=[whole(pltpu.SMEM)] + [whole(pltpu.HBM)] * 4,
        out_specs=(whole(), whole()),
        scratch_shapes=[pltpu.VMEM(w.shape, bf16) for w in weights]
        + [
            pltpu.SemaphoreType.DMA((2, len(pieces))),
            pltpu.VMEM(source.shape, bf16),
            pltpu.VMEM(scale.shape, bf16),
            pltpu.VMEM(source.shape, f32),
            pltpu.VMEM(source.shape, bf16),
            pltpu.SemaphoreType.DMA((2,)),
        ],
        compiler_params=pltpu.CompilerParams(vmem_limit_bytes=24 * MIB),
        cost_estimate=cost(2 * rows * width * message, 2 * width * message),
    )(own_index("tp"), far(source), far(scale), *map(far, weights))


def next_projection(normed, weights):
    shares, own, width = normed.shape
    message = sum(w.shape[1] for w in weights)

    def body(x, wq, wp, out):
        pieces = pieces_of(width, 8)
        store_shares(out, *project((wq, wp), lambda at, n: rows_of(x, at, n), shares * own, pieces))

    return call(
        body,
        jax.ShapeDtypeStruct((shares, own, message), bf16),
        [whole()] * 3,
        2 * shares * own * width * message,
        2 * width * message,
    )(normed, *weights)


def own_index(axis):
    return lax.axis_index(axis).astype(jnp.int32).reshape(1)


def fetch(block, per_block, slots, side, here, other, target, sem):
    stored_here = here.shape[0]
    slot = slots[per_block[block]]
    at = lax.rem(slot, jnp.int32(stored_here))
    mine = lax.div(slot, jnp.int32(stored_here)) == side[0]

    @pl.when(mine)
    def _():
        pltpu.make_async_copy(here.at[at], target.at[block], sem.at[block]).start()

    @pl.when(jnp.logical_not(mine))
    def _():
        pltpu.make_async_copy(other.at[at], target.at[block], sem.at[block]).start()

    return pltpu.make_async_copy(here.at[0], target.at[block], sem.at[block])


def add_down(message, adapters, here, other, lengths, blocks):
    shares, own, width = message.shape
    _, rank, columns = here.shape
    lead = rank // own * columns

    def body(per_block, slots, side, lens, m, here_ref, other_ref, out, turns, piece, sem):
        waits = [
            fetch(b, per_block, slots, side, here_ref, other_ref, piece, sem)
            for b in range(blocks)
        ]
        for j in range(shares):
            out[j, :, lead:] = m[j]
        half_head = HEAD_SIZE // 2
        lane = lax.broadcasted_iota(jnp.int32, (STEPS * own, HEAD_SIZE), 1)
        line = lax.broadcasted_iota(jnp.int32, (STEPS * own, HEAD_SIZE), 0)
        position = jnp.zeros_like(line)
        for n in range(STEPS * own):
            position = jnp.where(line == n, lens[n % own] + n // own, position)
        entry = jnp.where(lane < half_head, lane, lane - half_head).astype(f32)
        angle = position.astype(f32) * jnp.exp(entry * f32(-2.0 / HEAD_SIZE * math.log(rope_base)))
        sine = jnp.sin(angle)
        turns[0] = jnp.cos(angle)
        turns[1] = jnp.where(lane < half_head, -sine, sine)
        for wait in waits:
            wait.wait()
        for b in range(blocks):
            lines = [
                piece[b, m * own : (m + 1) * own, :].astype(f32) for m in range(rank // own)
            ]
            packed = jnp.concatenate(lines, axis=1).astype(bf16)
            for j in range(b * BLOCK // own, (b + 1) * BLOCK // own):
                out[j, :, :lead] = packed

    smem = whole(pltpu.SMEM)
    return pl.pallas_call(
        body,
        out_shape=(
            jax.ShapeDtypeStruct((shares, own, lead + width), bf16),
            jax.ShapeDtypeStruct((2, STEPS * own, HEAD_SIZE), f32),
        ),
        in_specs=[smem] * 4 + [whole(), whole(pl.ANY), whole(pl.ANY)],
        out_specs=(whole(), whole()),
        scratch_shapes=[
            pltpu.VMEM((blocks, rank, columns), bf16),
            pltpu.SemaphoreType.DMA((blocks,)),
        ],
        compiler_params=pltpu.CompilerParams(vmem_limit_bytes=16 * MIB),
    )(*adapters, lengths, message, here, other)


def attend(arrived, pairs, older, turns, lengths, cache, adapters, stores, step, lead, rank):
    shares, own, message = arrived.shape
    context, width = cache.shape[1:]
    half = width // 2
    query_width = QUERY_HEAD_COUNT * HEAD_SIZE // shares
    per_share = query_width // HEAD_SIZE
    groups = QUERY_HEAD_COUNT // KV_HEADS
    lines = groups * own
    pair_inside = pairs is None
    first, last = step == 0, step == STEPS - 1
    shrink = 1.0 / math.sqrt(HEAD_SIZE)

    def body(*refs):
        refs = list(refs)
        lens, x = refs.pop(0), refs.pop(0)
        pair_ref = None if pair_inside else refs.pop(0)
        old = None if first else refs.pop(0)
        turn_ref, kv = refs.pop(0), refs.pop(0)
        if first:
            per_block, slots, side, here, other, out, new, down_ref, ups, sem = refs
            waits = [
                fetch(b, per_block, slots, side, here, other, ups, sem)
                for b in range(ups.shape[0])
            ]
            for j in range(shares):
                pieces = [
                    x[j, :, m * query_width : (m + 1) * query_width].astype(f32)
                    for m in range(rank // own)
                ]
                down_ref[j] = jnp.concatenate(pieces, axis=0).astype(bf16)
        else:
            down_ref, out, new = refs
        cosine = turn_ref[0, step * own : (step + 1) * own, :]
        sine = turn_ref[1, step * own : (step + 1) * own, :]
        row_of = lax.rem(lax.broadcasted_iota(jnp.int32, (lines, 1), 0), own)

        def by_row(values):
            result = values[0]
            for r in range(1, own):
                result = jnp.where(row_of == r, values[r], result)
            return result

        def spread(rows):
            return by_row([rows[r : r + 1, :] for r in range(own)])

        def turn(v, c, s):
            return v * c + pltpu.roll(v, HEAD_SIZE // 2, 1) * s

        def pair_head(c):
            if pair_inside:
                return x[c, :, lead + query_width :].astype(f32)
            return pair_ref[:, c * HEAD_SIZE : (c + 1) * HEAD_SIZE].astype(f32)

        keys = [turn(pair_head(g), cosine, sine).astype(bf16) for g in range(KV_HEADS)]
        values = [pair_head(KV_HEADS + g).astype(bf16) for g in range(KV_HEADS)]
        fresh = jnp.concatenate(keys + values, axis=1)
        if last:
            new[0] = old[...]
            new[1] = fresh
        else:
            new[...] = fresh
        wide_cosine, wide_sine = spread(cosine), spread(sine)
        valid = lax.broadcasted_iota(jnp.int32, (lines, context), 1) < by_row(
            [jnp.full((lines, 1), lens[r], jnp.int32) for r in range(own)]
        )
        scores = []
        extras = []
        new_values = []
        for g in range(KV_HEADS):
            column = slice(g * HEAD_SIZE, (g + 1) * HEAD_SIZE)
            value_column = slice(half + g * HEAD_SIZE, half + (g + 1) * HEAD_SIZE)
            pieces = []
            for h in range(g * groups, (g + 1) * groups):
                at = lead + (h % per_share) * HEAD_SIZE
                pieces.append(x[h // per_share, :, at : at + HEAD_SIZE].astype(f32))
            query = turn(jnp.concatenate(pieces, axis=0), wide_cosine, wide_sine).astype(bf16)
            score = by_row(
                [
                    lax.dot_general(
                        query, kv[r, :, column], (((1,), (1,)), ((), ())), preferred_element_type=f32
                    )
                    for r in range(own)
                ]
            )
            scores.append(jnp.where(valid, score * shrink, f32(-1e30)))
            added = [(keys[g], values[g])]
            if not first:
                added.append((old[:, column], old[:, value_column]))
            wide_query = query.astype(f32)
            extras.append(
                [
                    jnp.sum(wide_query * spread(k.astype(f32)), axis=1, keepdims=True) * shrink
                    for k, _ in added
                ]
            )
            new_values.append([spread(v.astype(f32)) for _, v in added])
        results = []
        for g in range(KV_HEADS):
            value_column = slice(half + g * HEAD_SIZE, half + (g + 1) * HEAD_SIZE)
            peak = jnp.max(scores[g], axis=1, keepdims=True)
            for e in extras[g]:
                peak = jnp.maximum(peak, e)
            weight = jnp.exp(scores[g] - peak)
            more = [jnp.exp(e - peak) for e in extras[g]]
            total = jnp.sum(weight, axis=1, keepdims=True)
            for e in more:
                total = total + e
            probs = (weight / total).astype(bf16)
            result = by_row(
                [
                    jnp.dot(probs, kv[r, :, value_column], preferred_element_type=f32)
                    for r in range(own)
                ]
            )
            for e, v in zip(more, new_values[g]):
                result = result + (e / total).astype(bf16).astype(f32) * v
            results.append(result)
        low = jnp.zeros((own, rank), f32)
        for j in range(shares):
            cells = []
            for h in range(j * per_share, (j + 1) * per_share):
                at = h % groups * own
                cells.append(results[h // groups][at : at + own, :])
            share = jnp.concatenate(cells, axis=1).astype(bf16)
            out[j, :, :query_width] = share
            low = low + lax.dot_general(
                share, down_ref[j], (((1,), (1,)), ((), ())), preferred_element_type=f32
            )
        padded = jnp.concatenate([low, jnp.zeros((own, HEAD_SIZE - rank), f32)], axis=1).astype(bf16)
        for j in range(shares):
            out[j, :, query_width:] = padded
        if first:
            for wait in waits:
                wait.wait()

    smem = whole(pltpu.SMEM)
    operands = [lengths, arrived]
    specs = [smem, whole()]
    for extra in ([] if pair_inside else [pairs]) + ([] if first else [older]) + [turns, cache]:
        operands.append(extra)
        specs.append(whole())
    outs = [
        jax.ShapeDtypeStruct((shares, own, query_width + HEAD_SIZE), bf16),
        jax.ShapeDtypeStruct((STEPS, own, width) if last else (own, width), bf16),
    ]
    scratch = []
    if first:
        operands += [*adapters, far(stores[0]), stores[1]]
        specs += [smem] * 3 + [whole(pltpu.HBM), whole(pl.ANY)]
        blocks = adapters[0].shape[0]
        outs.append(jax.ShapeDtypeStruct((shares, rank, query_width), bf16))
        outs.append(jax.ShapeDtypeStruct((blocks,) + stores[0].shape[1:], bf16))
        scratch.append(pltpu.SemaphoreType.DMA((blocks,)))
    else:
        operands.append(stores)
        specs.append(whole())
    return pl.pallas_call(
        body,
        out_shape=tuple(outs),
        in_specs=specs,
        out_specs=(whole(),) * len(outs),
        scratch_shapes=scratch,
        compiler_params=pltpu.CompilerParams(vmem_limit_bytes=16 * MIB),
        cost_estimate=cost(
            8 * own * QUERY_HEAD_COUNT * HEAD_SIZE * context, 2 * own * context * width
        ),
    )(*operands)


def output_terms(arrived, output_weight, up):
    shares, own, _ = arrived.shape
    query_width, width = output_weight.shape
    blocks, rank, share_width = up.shape
    rows = shares * own
    step = 1024

    def body(mine, x, wo, up_ref, out, added):
        heads = rows_of(x, 0, query_width)
        low = rows_of(x, query_width, HEAD_SIZE)[:, :rank]
        added[...] = jnp.zeros_like(added)
        start = pl.multiple_of(mine[0] * share_width, share_width)
        for b in range(blocks):
            lines = slice(b * BLOCK, (b + 1) * BLOCK)
            added[lines, pl.ds(start, share_width)] = jnp.dot(
                low[lines], up_ref[b], preferred_element_type=f32
            )
        for i in range(width // step):
            columns = slice(i * step, (i + 1) * step)
            total = added[:, columns] + jnp.dot(
                heads, wo[:, columns], preferred_element_type=f32
            )
            for j in range(shares):
                out[j, :, columns] = total[j * own : (j + 1) * own, :].astype(out.dtype)

    return pl.pallas_call(
        body,
        out_shape=jax.ShapeDtypeStruct((shares, own, width), term_type),
        in_specs=[whole(pltpu.SMEM)] + [whole()] * 3,
        out_specs=whole(),
        scratch_shapes=[pltpu.VMEM((rows, width), f32)],
        compiler_params=pltpu.CompilerParams(vmem_limit_bytes=16 * MIB),
        cost_estimate=cost(2 * rows * width * query_width, 2 * width * query_width),
    )(own_index("tp"), arrived, output_weight, up)


def close_step(terms, hidden, scale):
    shares, own, width = terms.shape
    normed = scale is not None

    def body(t, h, *refs):
        total = h[...].astype(f32)
        for j in range(shares):
            total = total + t[j].astype(f32)
        rounded = total.astype(bf16)
        spread = rounded
        if normed:
            s, out, kept = refs
            kept[...] = rounded
            wide = rounded.astype(f32)
            mean = jnp.mean(wide * wide, axis=-1, keepdims=True)
            wide = wide * lax.rsqrt(mean + norm_epsilon)
            gain = s[...].astype(f32)
            spread = jnp.concatenate(
                [
                    wide[:, c * HEAD_SIZE : (c + 1) * HEAD_SIZE] * gain[c : c + 1, :]
                    for c in range(width // HEAD_SIZE)
                ],
                axis=1,
            ).astype(bf16)
        else:
            (out,) = refs
        for j in range(shares):
            out[j] = spread

    outs = [jax.ShapeDtypeStruct((shares, own, width), bf16)]
    operands = [terms, hidden]
    if normed:
        outs.append(jax.ShapeDtypeStruct((own, width), bf16))
        operands.append(scale)
    return call(
        body, tuple(outs), [whole()] * len(operands), 8 * own * width, 6 * shares * own * width
    )(*operands)


def exchange(chunks):
    return lax.all_to_all(chunks, "tp", split_axis=0, concat_axis=0, tiled=True)


def local(
    input_hidden_rows,
    input_norm_scale,
    query_weight,
    key_value_weight,
    output_weight,
    cache,
    lengths,
    adapter_per_block,
    adapter_storage_slot,
    adapter_down_projection,
    adapter_up_projection,
):
    rows_req = input_hidden_rows.shape[0]
    own = cache.shape[0]
    blocks = rows_req // BLOCK
    width = input_hidden_rows.shape[1]
    query_width = query_weight.shape[1]
    rank = adapter_down_projection.shape[1]
    scale = input_norm_scale.reshape(width // HEAD_SIZE, HEAD_SIZE)
    adapters = (
        adapter_per_block,
        adapter_storage_slot,
        own_index("req"),
    )
    cores = [(0, 1), (1, 0)]
    other_down = lax.ppermute(adapter_down_projection, "req", cores)
    other_up = lax.ppermute(adapter_up_projection, "req", cores)
    lead = rank // own * query_width
    weights = (query_weight, key_value_weight)
    message, hidden = first_projection(input_hidden_rows, scale, weights, own)
    message, turns = add_down(
        message, adapters, adapter_down_projection, other_down, lengths, blocks
    )
    down = fresh = None
    for step in range(STEPS):
        arrived = exchange(message)
        start = 0 if step else lead
        pairs = None
        if key_value_weight.shape[1] != HEAD_SIZE:
            pairs = arrived[:, :, start + query_width :].transpose(1, 0, 2).reshape(own, -1)
        stores = down if step else (adapter_up_projection, other_up)
        attended, fresh, *kept = attend(
            arrived, pairs, fresh, turns, lengths, cache, adapters, stores, step, start, rank
        )
        if not step:
            down, up = kept
        terms = exchange(output_terms(exchange(attended), output_weight, up))
        if step < STEPS - 1:
            spread, hidden = close_step(terms, hidden, scale)
            message = next_projection(exchange(spread), weights)
        else:
            (spread,) = close_step(terms, hidden, None)
    return (exchange(spread).reshape(rows_req, width), fresh)


def solution(mesh):
    in_specs = (
        P(("parts", "req"), None),
        P(),
        P(None, "tp"),
        P(None, "tp"),
        P("tp", None),
        P(("parts", "req", "tp"), None, None),
        P(("parts", "req", "tp")),
        P(("parts", "req")),
        P(),
        P("req", None, "tp"),
        P("req", None, "tp"),
    )
    out_specs = (P(("parts", "req"), None), P(None, ("parts", "req", "tp"), None))
    return jax.shard_map(local, mesh=mesh, in_specs=in_specs, out_specs=out_specs, check_vma=False)
```

```python
import math

import jax
import jax.numpy as jnp
from jax import lax
from jax.experimental import pallas as pl
from jax.experimental.pallas import tpu as pltpu
from jax.sharding import PartitionSpec as P

MODEL_WIDTH = 8192
HEAD_SIZE = 128
QUERY_HEAD_COUNT = 32
KV_HEADS = 4
BLOCK = 16
STEPS = 2

rope_base = 500000.0
norm_epsilon = 1e-05
term_type = jnp.bfloat16
f32 = jnp.float32
bf16 = jnp.bfloat16
MIB = 1 << 20


def whole(kind=pltpu.VMEM):
    return pl.BlockSpec(memory_space=kind)


def call(body, outs, ins, flops, data_bytes, limit=16):
    return pl.pallas_call(
        body,
        out_shape=outs,
        in_specs=ins,
        out_specs=jax.tree.map(lambda _: whole(), outs),
        compiler_params=pltpu.CompilerParams(vmem_limit_bytes=limit * MIB),
        cost_estimate=pl.CostEstimate(flops=flops, bytes_accessed=data_bytes, transcendentals=0),
    )


def far(array):
    return pltpu.with_memory_space_constraint(array, pltpu.HBM)


def rows_of(ref, start, width):
    pieces = [ref[j, :, pl.ds(start, width)].astype(f32) for j in range(ref.shape[0])]
    return jnp.concatenate(pieces, axis=0).astype(bf16)


def pieces_of(depth, count):
    return [(i * depth // count, (i + 1) * depth // count) for i in range(count)]


def project(weights, chunk_of, rows, pieces, ready=None):
    sums = [jnp.zeros((rows, w.shape[1]), f32) for w in weights]
    for i, (start, stop) in enumerate(pieces):
        if ready is not None:
            ready(i)
        part = chunk_of(start, stop - start)
        sums = [
            total + jnp.dot(part, w[start:stop, :], preferred_element_type=f32)
            for total, w in zip(sums, weights)
        ]
    return sums


def store_shares(out, query, pair):
    shares, own, _ = out.shape
    width = query.shape[1]
    for j in range(shares):
        lines = slice(j * own, (j + 1) * own)
        out[j, :, :width] = query[lines].astype(bf16)
        out[j, :, width:] = pair[lines].astype(bf16)


def cost(flops, data_bytes):
    return pl.CostEstimate(flops=flops, bytes_accessed=data_bytes, transcendentals=0)


def first_projection(source, scale, weights, own):
    rows, width = source.shape
    shares = rows // own
    message = sum(w.shape[1] for w in weights)
    pieces = pieces_of(width, 4)
    ahead = 2

    def body(mine, source_ref, s, wq, wp, out, held, *scratch):
        kept_q, kept_p, sems, x, gains, wide, normed, pre = scratch
        loads = [
            pltpu.make_async_copy(source_ref, x, pre.at[0]),
            pltpu.make_async_copy(s, gains, pre.at[1]),
        ]
        for load in loads:
            load.start()
        copies = [
            [
                pltpu.make_async_copy(w.at[start:stop, :], k.at[start:stop, :], sems.at[n, i])
                for n, (w, k) in enumerate(((wq, kept_q), (wp, kept_p)))
            ]
            for i, (start, stop) in enumerate(pieces)
        ]
        for pair in copies[:ahead]:
            for copy in pair:
                copy.start()

        def ready(i):
            for copy in copies[i]:
                copy.wait()
            for copy in copies[i + ahead] if i + ahead < len(copies) else []:
                copy.start()

        for load in loads:
            load.wait()
        wide[...] = x[...].astype(f32)
        lines = wide[:own, :]
        for j in range(1, shares):
            lines = jnp.where(mine[0] == j, wide[j * own : (j + 1) * own, :], lines)
        held[...] = lines.astype(bf16)
        value = wide[...]
        ratio = lax.rsqrt(jnp.mean(value * value, axis=-1, keepdims=True) + norm_epsilon)
        gain = gains[...].astype(f32)
        for c in range(width // HEAD_SIZE):
            columns = slice(c * HEAD_SIZE, (c + 1) * HEAD_SIZE)
            normed[:, columns] = (wide[:, columns] * ratio * gain[c : c + 1, :]).astype(bf16)
        sums = project(
            (kept_q, kept_p), lambda at, n: normed[:, at : at + n], rows, pieces, ready
        )
        store_shares(out, *sums)

    return pl.pallas_call(
        body,
        out_shape=(
            jax.ShapeDtypeStruct((shares, own, message), bf16),
            jax.ShapeDtypeStruct((own, width), bf16),
        ),
        in_specs=[whole(pltpu.SMEM)] + [whole(pltpu.HBM)] * 4,
        out_specs=(whole(), whole()),
        scratch_shapes=[pltpu.VMEM(w.shape, bf16) for w in weights]
        + [
            pltpu.SemaphoreType.DMA((2, len(pieces))),
            pltpu.VMEM(source.shape, bf16),
            pltpu.VMEM(scale.shape, bf16),
            pltpu.VMEM(source.shape, f32),
            pltpu.VMEM(source.shape, bf16),
            pltpu.SemaphoreType.DMA((2,)),
        ],
        compiler_params=pltpu.CompilerParams(vmem_limit_bytes=24 * MIB),
        cost_estimate=cost(2 * rows * width * message, 2 * width * message),
    )(own_index("tp"), far(source), far(scale), *map(far, weights))


def next_projection(normed, weights):
    shares, own, width = normed.shape
    message = sum(w.shape[1] for w in weights)

    def body(x, wq, wp, out):
        pieces = pieces_of(width, 8)
        store_shares(out, *project((wq, wp), lambda at, n: rows_of(x, at, n), shares * own, pieces))

    return call(
        body,
        jax.ShapeDtypeStruct((shares, own, message), bf16),
        [whole()] * 3,
        2 * shares * own * width * message,
        2 * width * message,
    )(normed, *weights)


def own_index(axis):
    return lax.axis_index(axis).astype(jnp.int32).reshape(1)


def fetch(block, per_block, slots, side, here, other, target, sem):
    stored_here = here.shape[0]
    slot = slots[per_block[block]]
    at = lax.rem(slot, jnp.int32(stored_here))
    mine = lax.div(slot, jnp.int32(stored_here)) == side[0]

    @pl.when(mine)
    def _():
        pltpu.make_async_copy(here.at[at], target.at[block], sem.at[block]).start()

    @pl.when(jnp.logical_not(mine))
    def _():
        pltpu.make_async_copy(other.at[at], target.at[block], sem.at[block]).start()

    return pltpu.make_async_copy(here.at[0], target.at[block], sem.at[block])


def add_down(message, adapters, here, other, lengths, blocks):
    shares, own, width = message.shape
    _, rank, columns = here.shape
    lead = rank // own * columns

    def body(per_block, slots, side, lens, m, here_ref, other_ref, out, turns, piece, sem):
        waits = [
            fetch(b, per_block, slots, side, here_ref, other_ref, piece, sem)
            for b in range(blocks)
        ]
        for j in range(shares):
            out[j, :, lead:] = m[j]
        half_head = HEAD_SIZE // 2
        lane = lax.broadcasted_iota(jnp.int32, (STEPS * own, HEAD_SIZE), 1)
        line = lax.broadcasted_iota(jnp.int32, (STEPS * own, HEAD_SIZE), 0)
        position = jnp.zeros_like(line)
        for n in range(STEPS * own):
            position = jnp.where(line == n, lens[n % own] + n // own, position)
        entry = jnp.where(lane < half_head, lane, lane - half_head).astype(f32)
        angle = position.astype(f32) * jnp.exp(entry * f32(-2.0 / HEAD_SIZE * math.log(rope_base)))
        sine = jnp.sin(angle)
        turns[0] = jnp.cos(angle)
        turns[1] = jnp.where(lane < half_head, -sine, sine)
        for wait in waits:
            wait.wait()
        for b in range(blocks):
            lines = [
                piece[b, m * own : (m + 1) * own, :].astype(f32) for m in range(rank // own)
            ]
            packed = jnp.concatenate(lines, axis=1).astype(bf16)
            for j in range(b * BLOCK // own, (b + 1) * BLOCK // own):
                out[j, :, :lead] = packed

    smem = whole(pltpu.SMEM)
    return pl.pallas_call(
        body,
        out_shape=(
            jax.ShapeDtypeStruct((shares, own, lead + width), bf16),
            jax.ShapeDtypeStruct((2, STEPS * own, HEAD_SIZE), f32),
        ),
        in_specs=[smem] * 4 + [whole(), whole(pl.ANY), whole(pl.ANY)],
        out_specs=(whole(), whole()),
        scratch_shapes=[
            pltpu.VMEM((blocks, rank, columns), bf16),
            pltpu.SemaphoreType.DMA((blocks,)),
        ],
        compiler_params=pltpu.CompilerParams(vmem_limit_bytes=16 * MIB),
    )(*adapters, lengths, message, here, other)


def attend(arrived, pairs, older, turns, lengths, cache, adapters, stores, step, lead, rank):
    shares, own, message = arrived.shape
    context, width = cache.shape[1:]
    half = width // 2
    query_width = QUERY_HEAD_COUNT * HEAD_SIZE // shares
    per_share = query_width // HEAD_SIZE
    groups = QUERY_HEAD_COUNT // KV_HEADS
    lines = groups * own
    pair_inside = pairs is None
    first = step == 0
    shrink = 1.0 / math.sqrt(HEAD_SIZE)

    def body(*refs):
        refs = list(refs)
        lens, x = refs.pop(0), refs.pop(0)
        pair_ref = None if pair_inside else refs.pop(0)
        old = None if first else refs.pop(0)
        turn_ref, kv = refs.pop(0), refs.pop(0)
        if first:
            per_block, slots, side, here, other, out, new, down_ref, ups, sem = refs
            waits = [
                fetch(b, per_block, slots, side, here, other, ups, sem)
                for b in range(ups.shape[0])
            ]
            for j in range(shares):
                pieces = [
                    x[j, :, m * query_width : (m + 1) * query_width].astype(f32)
                    for m in range(rank // own)
                ]
                down_ref[j] = jnp.concatenate(pieces, axis=0).astype(bf16)
        else:
            down_ref, out, new = refs
        cosine = turn_ref[0, step * own : (step + 1) * own, :]
        sine = turn_ref[1, step * own : (step + 1) * own, :]
        row_of = lax.rem(lax.broadcasted_iota(jnp.int32, (lines, 1), 0), own)

        def by_row(values):
            result = values[0]
            for r in range(1, own):
                result = jnp.where(row_of == r, values[r], result)
            return result

        def spread(rows):
            return by_row([rows[r : r + 1, :] for r in range(own)])

        def turn(v, c, s):
            return v * c + pltpu.roll(v, HEAD_SIZE // 2, 1) * s

        def pair_head(c):
            if pair_inside:
                return x[c, :, lead + query_width :].astype(f32)
            return pair_ref[:, c * HEAD_SIZE : (c + 1) * HEAD_SIZE].astype(f32)

        keys = [turn(pair_head(g), cosine, sine).astype(bf16) for g in range(KV_HEADS)]
        values = [pair_head(KV_HEADS + g).astype(bf16) for g in range(KV_HEADS)]
        fresh = jnp.concatenate(keys + values, axis=1)
        new[...] = fresh
        wide_cosine, wide_sine = spread(cosine), spread(sine)
        valid = lax.broadcasted_iota(jnp.int32, (lines, context), 1) < by_row(
            [jnp.full((lines, 1), lens[r], jnp.int32) for r in range(own)]
        )
        scores = []
        extras = []
        new_values = []
        for g in range(KV_HEADS):
            column = slice(g * HEAD_SIZE, (g + 1) * HEAD_SIZE)
            value_column = slice(half + g * HEAD_SIZE, half + (g + 1) * HEAD_SIZE)
            pieces = []
            for h in range(g * groups, (g + 1) * groups):
                at = lead + (h % per_share) * HEAD_SIZE
                pieces.append(x[h // per_share, :, at : at + HEAD_SIZE].astype(f32))
            query = turn(jnp.concatenate(pieces, axis=0), wide_cosine, wide_sine).astype(bf16)
            score = by_row(
                [
                    lax.dot_general(
                        query, kv[r, :, column], (((1,), (1,)), ((), ())), preferred_element_type=f32
                    )
                    for r in range(own)
                ]
            )
            scores.append(jnp.where(valid, score * shrink, f32(-1e30)))
            added = [(keys[g], values[g])]
            if not first:
                added.append((old[:, column], old[:, value_column]))
            wide_query = query.astype(f32)
            extras.append(
                [
                    jnp.sum(wide_query * spread(k.astype(f32)), axis=1, keepdims=True) * shrink
                    for k, _ in added
                ]
            )
            new_values.append([spread(v.astype(f32)) for _, v in added])
        results = []
        for g in range(KV_HEADS):
            value_column = slice(half + g * HEAD_SIZE, half + (g + 1) * HEAD_SIZE)
            peak = jnp.max(scores[g], axis=1, keepdims=True)
            for e in extras[g]:
                peak = jnp.maximum(peak, e)
            weight = jnp.exp(scores[g] - peak)
            more = [jnp.exp(e - peak) for e in extras[g]]
            total = jnp.sum(weight, axis=1, keepdims=True)
            for e in more:
                total = total + e
            probs = (weight / total).astype(bf16)
            result = by_row(
                [
                    jnp.dot(probs, kv[r, :, value_column], preferred_element_type=f32)
                    for r in range(own)
                ]
            )
            for e, v in zip(more, new_values[g]):
                result = result + (e / total).astype(bf16).astype(f32) * v
            results.append(result)
        low = jnp.zeros((own, rank), f32)
        for j in range(shares):
            cells = []
            for h in range(j * per_share, (j + 1) * per_share):
                at = h % groups * own
                cells.append(results[h // groups][at : at + own, :])
            share = jnp.concatenate(cells, axis=1).astype(bf16)
            out[j, :, :query_width] = share
            low = low + lax.dot_general(
                share, down_ref[j], (((1,), (1,)), ((), ())), preferred_element_type=f32
            )
        padded = jnp.concatenate([low, jnp.zeros((own, HEAD_SIZE - rank), f32)], axis=1).astype(bf16)
        for j in range(shares):
            out[j, :, query_width:] = padded
        if first:
            for wait in waits:
                wait.wait()

    smem = whole(pltpu.SMEM)
    operands = [lengths, arrived]
    specs = [smem, whole()]
    for extra in ([] if pair_inside else [pairs]) + ([] if first else [older]) + [turns, cache]:
        operands.append(extra)
        specs.append(whole())
    outs = [
        jax.ShapeDtypeStruct((shares, own, query_width + HEAD_SIZE), bf16),
        jax.ShapeDtypeStruct((own, width), bf16),
    ]
    scratch = []
    if first:
        operands += [*adapters, far(stores[0]), stores[1]]
        specs += [smem] * 3 + [whole(pltpu.HBM), whole(pl.ANY)]
        blocks = adapters[0].shape[0]
        outs.append(jax.ShapeDtypeStruct((shares, rank, query_width), bf16))
        outs.append(jax.ShapeDtypeStruct((blocks,) + stores[0].shape[1:], bf16))
        scratch.append(pltpu.SemaphoreType.DMA((blocks,)))
    else:
        operands.append(stores)
        specs.append(whole())
    return pl.pallas_call(
        body,
        out_shape=tuple(outs),
        in_specs=specs,
        out_specs=(whole(),) * len(outs),
        scratch_shapes=scratch,
        compiler_params=pltpu.CompilerParams(vmem_limit_bytes=16 * MIB),
        cost_estimate=cost(
            8 * own * QUERY_HEAD_COUNT * HEAD_SIZE * context, 2 * own * context * width
        ),
    )(*operands)


def output_terms(arrived, output_weight, up, pairs):
    shares, own, _ = arrived.shape
    query_width, width = output_weight.shape
    blocks, rank, share_width = up.shape
    rows = shares * own
    step = 1024

    count = len(pairs)

    def body(mine, x, wo, up_ref, *refs):
        given, refs = refs[:count], refs[count:]
        out, added = refs[0], refs[1 + bool(count)]
        copies = [
            pltpu.make_async_copy(pair, refs[1].at[n], refs[3].at[n])
            for n, pair in enumerate(given)
        ]
        for copy in copies:
            copy.start()
        heads = rows_of(x, 0, query_width)
        low = rows_of(x, query_width, HEAD_SIZE)[:, :rank]
        added[...] = jnp.zeros_like(added)
        start = pl.multiple_of(mine[0] * share_width, share_width)
        for b in range(blocks):
            lines = slice(b * BLOCK, (b + 1) * BLOCK)
            added[lines, pl.ds(start, share_width)] = jnp.dot(
                low[lines], up_ref[b], preferred_element_type=f32
            )
        for i in range(width // step):
            columns = slice(i * step, (i + 1) * step)
            total = added[:, columns] + jnp.dot(
                heads, wo[:, columns], preferred_element_type=f32
            )
            for j in range(shares):
                out[j, :, columns] = total[j * own : (j + 1) * own, :].astype(out.dtype)
        for copy in copies:
            copy.wait()

    outs = [jax.ShapeDtypeStruct((shares, own, width), term_type)]
    out_specs = [whole()]
    scratch = [pltpu.VMEM((rows, width), f32)]
    if count:
        outs.append(jax.ShapeDtypeStruct((count,) + pairs[0].shape, bf16))
        out_specs.append(whole(pltpu.HBM))
        scratch.append(pltpu.SemaphoreType.DMA((count,)))
    return pl.pallas_call(
        body,
        out_shape=tuple(outs),
        in_specs=[whole(pltpu.SMEM)] + [whole()] * 3 + [whole(pl.ANY)] * count,
        out_specs=tuple(out_specs),
        scratch_shapes=scratch,
        compiler_params=pltpu.CompilerParams(vmem_limit_bytes=16 * MIB),
        cost_estimate=cost(2 * rows * width * query_width, 2 * width * query_width),
    )(own_index("tp"), arrived, output_weight, up, *pairs)


def close_step(terms, hidden, scale):
    shares, own, width = terms.shape
    normed = scale is not None

    def body(t, h, *refs):
        total = h[...].astype(f32)
        for j in range(shares):
            total = total + t[j].astype(f32)
        rounded = total.astype(bf16)
        spread = rounded
        if normed:
            s, out, kept = refs
            kept[...] = rounded
            wide = rounded.astype(f32)
            mean = jnp.mean(wide * wide, axis=-1, keepdims=True)
            wide = wide * lax.rsqrt(mean + norm_epsilon)
            gain = s[...].astype(f32)
            spread = jnp.concatenate(
                [
                    wide[:, c * HEAD_SIZE : (c + 1) * HEAD_SIZE] * gain[c : c + 1, :]
                    for c in range(width // HEAD_SIZE)
                ],
                axis=1,
            ).astype(bf16)
        else:
            (out,) = refs
        for j in range(shares):
            out[j] = spread

    outs = [jax.ShapeDtypeStruct((shares, own, width), bf16)]
    operands = [terms, hidden]
    if normed:
        outs.append(jax.ShapeDtypeStruct((own, width), bf16))
        operands.append(scale)
    return call(
        body, tuple(outs), [whole()] * len(operands), 8 * own * width, 6 * shares * own * width
    )(*operands)


def exchange(chunks):
    return lax.all_to_all(chunks, "tp", split_axis=0, concat_axis=0, tiled=True)


def local(
    input_hidden_rows,
    input_norm_scale,
    query_weight,
    key_value_weight,
    output_weight,
    cache,
    lengths,
    adapter_per_block,
    adapter_storage_slot,
    adapter_down_projection,
    adapter_up_projection,
):
    rows_req = input_hidden_rows.shape[0]
    own = cache.shape[0]
    blocks = rows_req // BLOCK
    width = input_hidden_rows.shape[1]
    query_width = query_weight.shape[1]
    rank = adapter_down_projection.shape[1]
    scale = input_norm_scale.reshape(width // HEAD_SIZE, HEAD_SIZE)
    adapters = (
        adapter_per_block,
        adapter_storage_slot,
        own_index("req"),
    )
    cores = [(0, 1), (1, 0)]
    other_down = lax.ppermute(adapter_down_projection, "req", cores)
    other_up = lax.ppermute(adapter_up_projection, "req", cores)
    lead = rank // own * query_width
    weights = (query_weight, key_value_weight)
    message, hidden = first_projection(input_hidden_rows, scale, weights, own)
    message, turns = add_down(
        message, adapters, adapter_down_projection, other_down, lengths, blocks
    )
    down = fresh = None
    made = []
    for step in range(STEPS):
        arrived = exchange(message)
        start = 0 if step else lead
        pairs = None
        if key_value_weight.shape[1] != HEAD_SIZE:
            pairs = arrived[:, :, start + query_width :].transpose(1, 0, 2).reshape(own, -1)
        stores = down if step else (adapter_up_projection, other_up)
        attended, fresh, *kept = attend(
            arrived, pairs, fresh, turns, lengths, cache, adapters, stores, step, start, rank
        )
        if not step:
            down, up = kept
        made.append(fresh)
        terms, *new_pairs = output_terms(
            exchange(attended), output_weight, up, made if step == STEPS - 1 else []
        )
        terms = exchange(terms)
        if step < STEPS - 1:
            spread, hidden = close_step(terms, hidden, scale)
            message = next_projection(exchange(spread), weights)
        else:
            (spread,) = close_step(terms, hidden, None)
    return (exchange(spread).reshape(rows_req, width), new_pairs[0])


def solution(mesh):
    in_specs = (
        P(("parts", "req"), None),
        P(),
        P(None, "tp"),
        P(None, "tp"),
        P("tp", None),
        P(("parts", "req", "tp"), None, None),
        P(("parts", "req", "tp")),
        P(("parts", "req")),
        P(),
        P("req", None, "tp"),
        P("req", None, "tp"),
    )
    out_specs = (P(("parts", "req"), None), P(None, ("parts", "req", "tp"), None))
    return jax.shard_map(local, mesh=mesh, in_specs=in_specs, out_specs=out_specs, check_vma=False)
```

```python
import math

import jax
import jax.numpy as jnp
from jax import lax
from jax.experimental import pallas as pl
from jax.experimental.pallas import tpu as pltpu
from jax.sharding import PartitionSpec as P

MODEL_WIDTH = 8192
HEAD_SIZE = 128
QUERY_HEAD_COUNT = 32
KV_HEADS = 4
BLOCK = 16
STEPS = 2

rope_base = 500000.0
norm_epsilon = 1e-05
term_type = jnp.bfloat16
f32 = jnp.float32
bf16 = jnp.bfloat16
MIB = 1 << 20


def whole(kind=pltpu.VMEM):
    return pl.BlockSpec(memory_space=kind)


def call(body, outs, ins, flops, data_bytes, limit=16):
    return pl.pallas_call(
        body,
        out_shape=outs,
        in_specs=ins,
        out_specs=jax.tree.map(lambda _: whole(), outs),
        compiler_params=pltpu.CompilerParams(vmem_limit_bytes=limit * MIB),
        cost_estimate=pl.CostEstimate(flops=flops, bytes_accessed=data_bytes, transcendentals=0),
    )


def far(array):
    return pltpu.with_memory_space_constraint(array, pltpu.HBM)


def rows_of(ref, start, width):
    pieces = [ref[j, :, pl.ds(start, width)].astype(f32) for j in range(ref.shape[0])]
    return jnp.concatenate(pieces, axis=0).astype(bf16)


def pieces_of(depth, count):
    return [(i * depth // count, (i + 1) * depth // count) for i in range(count)]


def project(weights, chunk_of, rows, pieces, ready=None):
    sums = [jnp.zeros((rows, w.shape[1]), f32) for w in weights]
    for i, (start, stop) in enumerate(pieces):
        if ready is not None:
            ready(i)
        part = chunk_of(start, stop - start)
        sums = [
            total + jnp.dot(part, w[start:stop, :], preferred_element_type=f32)
            for total, w in zip(sums, weights)
        ]
    return sums


def store_shares(out, query, pair):
    shares, own, _ = out.shape
    width = query.shape[1]
    for j in range(shares):
        lines = slice(j * own, (j + 1) * own)
        out[j, :, :width] = query[lines].astype(bf16)
        out[j, :, width:] = pair[lines].astype(bf16)


def cost(flops, data_bytes):
    return pl.CostEstimate(flops=flops, bytes_accessed=data_bytes, transcendentals=0)


def first_projection(source, scale, weights, own):
    rows, width = source.shape
    shares = rows // own
    message = sum(w.shape[1] for w in weights)
    pieces = pieces_of(width, 4)
    ahead = 3

    def body(mine, source_ref, s, wq, wp, out, held, *scratch):
        kept_q, kept_p, sems, x, gains, wide, normed, pre = scratch
        loads = [
            pltpu.make_async_copy(source_ref, x, pre.at[0]),
            pltpu.make_async_copy(s, gains, pre.at[1]),
        ]
        for load in loads:
            load.start()
        copies = [
            [
                pltpu.make_async_copy(w.at[start:stop, :], k.at[start:stop, :], sems.at[n, i])
                for n, (w, k) in enumerate(((wq, kept_q), (wp, kept_p)))
            ]
            for i, (start, stop) in enumerate(pieces)
        ]
        for pair in copies[:ahead]:
            for copy in pair:
                copy.start()

        def ready(i):
            for copy in copies[i]:
                copy.wait()
            for copy in copies[i + ahead] if i + ahead < len(copies) else []:
                copy.start()

        for load in loads:
            load.wait()
        wide[...] = x[...].astype(f32)
        lines = wide[:own, :]
        for j in range(1, shares):
            lines = jnp.where(mine[0] == j, wide[j * own : (j + 1) * own, :], lines)
        held[...] = lines.astype(bf16)
        value = wide[...]
        ratio = lax.rsqrt(jnp.mean(value * value, axis=-1, keepdims=True) + norm_epsilon)
        gain = gains[...].astype(f32)
        for c in range(width // HEAD_SIZE):
            columns = slice(c * HEAD_SIZE, (c + 1) * HEAD_SIZE)
            normed[:, columns] = (wide[:, columns] * ratio * gain[c : c + 1, :]).astype(bf16)
        sums = project(
            (kept_q, kept_p), lambda at, n: normed[:, at : at + n], rows, pieces, ready
        )
        store_shares(out, *sums)

    return pl.pallas_call(
        body,
        out_shape=(
            jax.ShapeDtypeStruct((shares, own, message), bf16),
            jax.ShapeDtypeStruct((own, width), bf16),
        ),
        in_specs=[whole(pltpu.SMEM)] + [whole(pltpu.HBM)] * 4,
        out_specs=(whole(), whole()),
        scratch_shapes=[pltpu.VMEM(w.shape, bf16) for w in weights]
        + [
            pltpu.SemaphoreType.DMA((2, len(pieces))),
            pltpu.VMEM(source.shape, bf16),
            pltpu.VMEM(scale.shape, bf16),
            pltpu.VMEM(source.shape, f32),
            pltpu.VMEM(source.shape, bf16),
            pltpu.SemaphoreType.DMA((2,)),
        ],
        compiler_params=pltpu.CompilerParams(vmem_limit_bytes=24 * MIB),
        cost_estimate=cost(2 * rows * width * message, 2 * width * message),
    )(own_index("tp"), far(source), far(scale), *map(far, weights))


def next_projection(normed, weights):
    shares, own, width = normed.shape
    message = sum(w.shape[1] for w in weights)

    def body(x, wq, wp, out):
        pieces = pieces_of(width, 8)
        store_shares(out, *project((wq, wp), lambda at, n: rows_of(x, at, n), shares * own, pieces))

    return call(
        body,
        jax.ShapeDtypeStruct((shares, own, message), bf16),
        [whole()] * 3,
        2 * shares * own * width * message,
        2 * width * message,
    )(normed, *weights)


def own_index(axis):
    return lax.axis_index(axis).astype(jnp.int32).reshape(1)


def fetch(block, per_block, slots, side, here, other, target, sem):
    stored_here = here.shape[0]
    slot = slots[per_block[block]]
    at = lax.rem(slot, jnp.int32(stored_here))
    mine = lax.div(slot, jnp.int32(stored_here)) == side[0]

    @pl.when(mine)
    def _():
        pltpu.make_async_copy(here.at[at], target.at[block], sem.at[block]).start()

    @pl.when(jnp.logical_not(mine))
    def _():
        pltpu.make_async_copy(other.at[at], target.at[block], sem.at[block]).start()

    return pltpu.make_async_copy(here.at[0], target.at[block], sem.at[block])


def add_down(message, adapters, here, other, lengths, blocks):
    shares, own, width = message.shape
    _, rank, columns = here.shape
    lead = rank // own * columns

    def body(per_block, slots, side, lens, m, here_ref, other_ref, out, turns, piece, sem):
        waits = [
            fetch(b, per_block, slots, side, here_ref, other_ref, piece, sem)
            for b in range(blocks)
        ]
        for j in range(shares):
            out[j, :, lead:] = m[j]
        half_head = HEAD_SIZE // 2
        lane = lax.broadcasted_iota(jnp.int32, (STEPS * own, HEAD_SIZE), 1)
        line = lax.broadcasted_iota(jnp.int32, (STEPS * own, HEAD_SIZE), 0)
        position = jnp.zeros_like(line)
        for n in range(STEPS * own):
            position = jnp.where(line == n, lens[n % own] + n // own, position)
        entry = jnp.where(lane < half_head, lane, lane - half_head).astype(f32)
        angle = position.astype(f32) * jnp.exp(entry * f32(-2.0 / HEAD_SIZE * math.log(rope_base)))
        sine = jnp.sin(angle)
        turns[0] = jnp.cos(angle)
        turns[1] = jnp.where(lane < half_head, -sine, sine)
        for wait in waits:
            wait.wait()
        for b in range(blocks):
            lines = [
                piece[b, m * own : (m + 1) * own, :].astype(f32) for m in range(rank // own)
            ]
            packed = jnp.concatenate(lines, axis=1).astype(bf16)
            for j in range(b * BLOCK // own, (b + 1) * BLOCK // own):
                out[j, :, :lead] = packed

    smem = whole(pltpu.SMEM)
    return pl.pallas_call(
        body,
        out_shape=(
            jax.ShapeDtypeStruct((shares, own, lead + width), bf16),
            jax.ShapeDtypeStruct((2, STEPS * own, HEAD_SIZE), f32),
        ),
        in_specs=[smem] * 4 + [whole(), whole(pl.ANY), whole(pl.ANY)],
        out_specs=(whole(), whole()),
        scratch_shapes=[
            pltpu.VMEM((blocks, rank, columns), bf16),
            pltpu.SemaphoreType.DMA((blocks,)),
        ],
        compiler_params=pltpu.CompilerParams(vmem_limit_bytes=16 * MIB),
    )(*adapters, lengths, message, here, other)


def attend(arrived, pairs, older, turns, lengths, cache, adapters, stores, step, lead, rank):
    shares, own, message = arrived.shape
    context, width = cache.shape[1:]
    half = width // 2
    query_width = QUERY_HEAD_COUNT * HEAD_SIZE // shares
    per_share = query_width // HEAD_SIZE
    groups = QUERY_HEAD_COUNT // KV_HEADS
    lines = groups * own
    pair_inside = pairs is None
    first = step == 0
    shrink = 1.0 / math.sqrt(HEAD_SIZE)

    def body(*refs):
        refs = list(refs)
        lens, x = refs.pop(0), refs.pop(0)
        pair_ref = None if pair_inside else refs.pop(0)
        old = None if first else refs.pop(0)
        turn_ref, kv = refs.pop(0), refs.pop(0)
        if first:
            per_block, slots, side, here, other, out, new, down_ref, ups, sem = refs
            waits = [
                fetch(b, per_block, slots, side, here, other, ups, sem)
                for b in range(ups.shape[0])
            ]
            for j in range(shares):
                pieces = [
                    x[j, :, m * query_width : (m + 1) * query_width].astype(f32)
                    for m in range(rank // own)
                ]
                down_ref[j] = jnp.concatenate(pieces, axis=0).astype(bf16)
        else:
            down_ref, out, new = refs
        cosine = turn_ref[0, step * own : (step + 1) * own, :]
        sine = turn_ref[1, step * own : (step + 1) * own, :]
        row_of = lax.rem(lax.broadcasted_iota(jnp.int32, (lines, 1), 0), own)

        def by_row(values):
            result = values[0]
            for r in range(1, own):
                result = jnp.where(row_of == r, values[r], result)
            return result

        def spread(rows):
            return by_row([rows[r : r + 1, :] for r in range(own)])

        def turn(v, c, s):
            return v * c + pltpu.roll(v, HEAD_SIZE // 2, 1) * s

        def pair_head(c):
            if pair_inside:
                return x[c, :, lead + query_width :].astype(f32)
            return pair_ref[:, c * HEAD_SIZE : (c + 1) * HEAD_SIZE].astype(f32)

        keys = [turn(pair_head(g), cosine, sine).astype(bf16) for g in range(KV_HEADS)]
        values = [pair_head(KV_HEADS + g).astype(bf16) for g in range(KV_HEADS)]
        fresh = jnp.concatenate(keys + values, axis=1)
        new[...] = fresh
        wide_cosine, wide_sine = spread(cosine), spread(sine)
        valid = lax.broadcasted_iota(jnp.int32, (lines, context), 1) < by_row(
            [jnp.full((lines, 1), lens[r], jnp.int32) for r in range(own)]
        )
        scores = []
        extras = []
        new_values = []
        for g in range(KV_HEADS):
            column = slice(g * HEAD_SIZE, (g + 1) * HEAD_SIZE)
            value_column = slice(half + g * HEAD_SIZE, half + (g + 1) * HEAD_SIZE)
            pieces = []
            for h in range(g * groups, (g + 1) * groups):
                at = lead + (h % per_share) * HEAD_SIZE
                pieces.append(x[h // per_share, :, at : at + HEAD_SIZE].astype(f32))
            query = turn(jnp.concatenate(pieces, axis=0), wide_cosine, wide_sine).astype(bf16)
            score = by_row(
                [
                    lax.dot_general(
                        query, kv[r, :, column], (((1,), (1,)), ((), ())), preferred_element_type=f32
                    )
                    for r in range(own)
                ]
            )
            scores.append(jnp.where(valid, score * shrink, f32(-1e30)))
            added = [(keys[g], values[g])]
            if not first:
                added.append((old[:, column], old[:, value_column]))
            wide_query = query.astype(f32)
            extras.append(
                [
                    jnp.sum(wide_query * spread(k.astype(f32)), axis=1, keepdims=True) * shrink
                    for k, _ in added
                ]
            )
            new_values.append([spread(v.astype(f32)) for _, v in added])
        results = []
        for g in range(KV_HEADS):
            value_column = slice(half + g * HEAD_SIZE, half + (g + 1) * HEAD_SIZE)
            peak = jnp.max(scores[g], axis=1, keepdims=True)
            for e in extras[g]:
                peak = jnp.maximum(peak, e)
            weight = jnp.exp(scores[g] - peak)
            more = [jnp.exp(e - peak) for e in extras[g]]
            total = jnp.sum(weight, axis=1, keepdims=True)
            for e in more:
                total = total + e
            probs = (weight / total).astype(bf16)
            result = by_row(
                [
                    jnp.dot(probs, kv[r, :, value_column], preferred_element_type=f32)
                    for r in range(own)
                ]
            )
            for e, v in zip(more, new_values[g]):
                result = result + (e / total).astype(bf16).astype(f32) * v
            results.append(result)
        low = jnp.zeros((own, rank), f32)
        for j in range(shares):
            cells = []
            for h in range(j * per_share, (j + 1) * per_share):
                at = h % groups * own
                cells.append(results[h // groups][at : at + own, :])
            share = jnp.concatenate(cells, axis=1).astype(bf16)
            out[j, :, :query_width] = share
            low = low + lax.dot_general(
                share, down_ref[j], (((1,), (1,)), ((), ())), preferred_element_type=f32
            )
        padded = jnp.concatenate([low, jnp.zeros((own, HEAD_SIZE - rank), f32)], axis=1).astype(bf16)
        for j in range(shares):
            out[j, :, query_width:] = padded
        if first:
            for wait in waits:
                wait.wait()

    smem = whole(pltpu.SMEM)
    operands = [lengths, arrived]
    specs = [smem, whole()]
    for extra in ([] if pair_inside else [pairs]) + ([] if first else [older]) + [turns, cache]:
        operands.append(extra)
        specs.append(whole())
    outs = [
        jax.ShapeDtypeStruct((shares, own, query_width + HEAD_SIZE), bf16),
        jax.ShapeDtypeStruct((own, width), bf16),
    ]
    scratch = []
    if first:
        operands += [*adapters, far(stores[0]), stores[1]]
        specs += [smem] * 3 + [whole(pltpu.HBM), whole(pl.ANY)]
        blocks = adapters[0].shape[0]
        outs.append(jax.ShapeDtypeStruct((shares, rank, query_width), bf16))
        outs.append(jax.ShapeDtypeStruct((blocks,) + stores[0].shape[1:], bf16))
        scratch.append(pltpu.SemaphoreType.DMA((blocks,)))
    else:
        operands.append(stores)
        specs.append(whole())
    return pl.pallas_call(
        body,
        out_shape=tuple(outs),
        in_specs=specs,
        out_specs=(whole(),) * len(outs),
        scratch_shapes=scratch,
        compiler_params=pltpu.CompilerParams(vmem_limit_bytes=16 * MIB),
        cost_estimate=cost(
            8 * own * QUERY_HEAD_COUNT * HEAD_SIZE * context, 2 * own * context * width
        ),
    )(*operands)


def output_terms(arrived, output_weight, up, pairs):
    shares, own, _ = arrived.shape
    query_width, width = output_weight.shape
    blocks, rank, share_width = up.shape
    rows = shares * own
    step = 1024

    count = len(pairs)

    def body(mine, x, wo, up_ref, *refs):
        given, refs = refs[:count], refs[count:]
        out, added = refs[0], refs[1 + bool(count)]
        copies = [
            pltpu.make_async_copy(pair, refs[1].at[n], refs[3].at[n])
            for n, pair in enumerate(given)
        ]
        for copy in copies:
            copy.start()
        heads = rows_of(x, 0, query_width)
        low = rows_of(x, query_width, HEAD_SIZE)[:, :rank]
        added[...] = jnp.zeros_like(added)
        start = pl.multiple_of(mine[0] * share_width, share_width)
        for b in range(blocks):
            lines = slice(b * BLOCK, (b + 1) * BLOCK)
            added[lines, pl.ds(start, share_width)] = jnp.dot(
                low[lines], up_ref[b], preferred_element_type=f32
            )
        for i in range(width // step):
            columns = slice(i * step, (i + 1) * step)
            total = added[:, columns] + jnp.dot(
                heads, wo[:, columns], preferred_element_type=f32
            )
            for j in range(shares):
                out[j, :, columns] = total[j * own : (j + 1) * own, :].astype(out.dtype)
        for copy in copies:
            copy.wait()

    outs = [jax.ShapeDtypeStruct((shares, own, width), term_type)]
    out_specs = [whole()]
    scratch = [pltpu.VMEM((rows, width), f32)]
    if count:
        outs.append(jax.ShapeDtypeStruct((count,) + pairs[0].shape, bf16))
        out_specs.append(whole(pltpu.HBM))
        scratch.append(pltpu.SemaphoreType.DMA((count,)))
    return pl.pallas_call(
        body,
        out_shape=tuple(outs),
        in_specs=[whole(pltpu.SMEM)] + [whole()] * 3 + [whole(pl.ANY)] * count,
        out_specs=tuple(out_specs),
        scratch_shapes=scratch,
        compiler_params=pltpu.CompilerParams(vmem_limit_bytes=16 * MIB),
        cost_estimate=cost(2 * rows * width * query_width, 2 * width * query_width),
    )(own_index("tp"), arrived, output_weight, up, *pairs)


def close_step(terms, hidden, scale):
    shares, own, width = terms.shape
    normed = scale is not None

    def body(t, h, *refs):
        total = h[...].astype(f32)
        for j in range(shares):
            total = total + t[j].astype(f32)
        rounded = total.astype(bf16)
        spread = rounded
        if normed:
            s, out, kept = refs
            kept[...] = rounded
            wide = rounded.astype(f32)
            mean = jnp.mean(wide * wide, axis=-1, keepdims=True)
            wide = wide * lax.rsqrt(mean + norm_epsilon)
            gain = s[...].astype(f32)
            spread = jnp.concatenate(
                [
                    wide[:, c * HEAD_SIZE : (c + 1) * HEAD_SIZE] * gain[c : c + 1, :]
                    for c in range(width // HEAD_SIZE)
                ],
                axis=1,
            ).astype(bf16)
        else:
            (out,) = refs
        for j in range(shares):
            out[j] = spread

    outs = [jax.ShapeDtypeStruct((shares, own, width), bf16)]
    operands = [terms, hidden]
    if normed:
        outs.append(jax.ShapeDtypeStruct((own, width), bf16))
        operands.append(scale)
    return call(
        body, tuple(outs), [whole()] * len(operands), 8 * own * width, 6 * shares * own * width
    )(*operands)


def exchange(chunks):
    return lax.all_to_all(chunks, "tp", split_axis=0, concat_axis=0, tiled=True)


def local(
    input_hidden_rows,
    input_norm_scale,
    query_weight,
    key_value_weight,
    output_weight,
    cache,
    lengths,
    adapter_per_block,
    adapter_storage_slot,
    adapter_down_projection,
    adapter_up_projection,
):
    rows_req = input_hidden_rows.shape[0]
    own = cache.shape[0]
    blocks = rows_req // BLOCK
    width = input_hidden_rows.shape[1]
    query_width = query_weight.shape[1]
    rank = adapter_down_projection.shape[1]
    scale = input_norm_scale.reshape(width // HEAD_SIZE, HEAD_SIZE)
    adapters = (
        adapter_per_block,
        adapter_storage_slot,
        own_index("req"),
    )
    cores = [(0, 1), (1, 0)]
    other_down = lax.ppermute(adapter_down_projection, "req", cores)
    other_up = lax.ppermute(adapter_up_projection, "req", cores)
    lead = rank // own * query_width
    weights = (query_weight, key_value_weight)
    message, hidden = first_projection(input_hidden_rows, scale, weights, own)
    message, turns = add_down(
        message, adapters, adapter_down_projection, other_down, lengths, blocks
    )
    down = fresh = None
    made = []
    for step in range(STEPS):
        arrived = exchange(message)
        start = 0 if step else lead
        pairs = None
        if key_value_weight.shape[1] != HEAD_SIZE:
            pairs = arrived[:, :, start + query_width :].transpose(1, 0, 2).reshape(own, -1)
        stores = down if step else (adapter_up_projection, other_up)
        attended, fresh, *kept = attend(
            arrived, pairs, fresh, turns, lengths, cache, adapters, stores, step, start, rank
        )
        if not step:
            down, up = kept
        made.append(fresh)
        terms, *new_pairs = output_terms(
            exchange(attended), output_weight, up, made if step == STEPS - 1 else []
        )
        terms = exchange(terms)
        if step < STEPS - 1:
            spread, hidden = close_step(terms, hidden, scale)
            message = next_projection(exchange(spread), weights)
        else:
            (spread,) = close_step(terms, hidden, None)
    return (exchange(spread).reshape(rows_req, width), new_pairs[0])


def solution(mesh):
    in_specs = (
        P(("parts", "req"), None),
        P(),
        P(None, "tp"),
        P(None, "tp"),
        P("tp", None),
        P(("parts", "req", "tp"), None, None),
        P(("parts", "req", "tp")),
        P(("parts", "req")),
        P(),
        P("req", None, "tp"),
        P("req", None, "tp"),
    )
    out_specs = (P(("parts", "req"), None), P(None, ("parts", "req", "tp"), None))
    return jax.shard_map(local, mesh=mesh, in_specs=in_specs, out_specs=out_specs, check_vma=False)
```
